256 devices in a mesh: lat: 8 (over y, x_lo), lon: 32 (over z, x_hi, core).
Axes of the slice: x: 4 (x_hi: 2, x_lo: 2; x = x_hi * 2 + x_lo), y: 4, z: 8, core: 2. Of those that a mesh axis runs over, the one named last changes fastest.
Arguments:
- fine_tokens: bfloat16 [2, 48, 768, 512], P(None, 'lat', 'lon'), may hold values from -6 to 6
- grad_out: bfloat16 [2, 48, 768, 512], P(None, 'lat', 'lon'), may hold values from -6 to 6
- window_class: int32 [2, 48, 768], P(None, 'lat', 'lon'), may hold values from 0 to 2
- temper_fine: float32 [8], replicated, may hold values from 4 to 20
- temper_coarse: float32 [16], replicated, may hold values from 4 to 20
- gain_fine: float32 [512], replicated, may hold values from 0.1 to 1.9
- fine_qkv: bfloat16 [512, 1536], P('lon'), may hold values from -0.25 to 0.25
- fine_out: bfloat16 [512, 512], P('lon'), may hold values from -0.25 to 0.25
- gain_merge: float32 [2048], replicated, may hold values from 0.1 to 1.9
- merge_weight: bfloat16 [2048, 1024], P('lon'), may hold values from -0.125 to 0.125
- gain_coarse: float32 [1024], replicated, may hold values from 0.1 to 1.9
- coarse_qkv: bfloat16 [1024, 3072], P('lon'), may hold values from -0.1875 to 0.1875
- coarse_out: bfloat16 [1024, 1024], P('lon'), may hold values from -0.1875 to 0.1875
- split_weight: bfloat16 [1024, 2048], P('lon'), may hold values from -0.1875 to 0.1875
Outputs:
- output: bfloat16 [2, 48, 768, 512], P(None, 'lat', 'lon')
- grad_in: bfloat16 [2, 48, 768, 512], P(None, 'lat', 'lon')
The draws below stay inside these ranges and needn't reach their ends.
All inputs are finite; a program needn't handle non-finite values.
Results may differ from the reference program's by a relative error of at most 0.035.
Values may be sent and summed in bfloat16 or wider, within the bound.
A program may use at most 128 MiB of HBM per device.

```python
import math
import jax
import jax.numpy as jnp
from jax import lax

D = 512
DC = 1024
HF = 8
HC = 16
LEV = 2
WL = 2
WLAT = 6
WLON = 12
SLAT = 3
SLON = 6
NLAT = 48
NLON = 768


def place_ends(drawn, rng, smallest, high):
    index_at = [jax.random.randint(jax.random.fold_in(rng, axis), (), 0, length) for axis, length in enumerate(drawn.shape)]
    main_axis = drawn.shape.index(max(drawn.shape))
    neighbour = index_at[:main_axis] + [(index_at[main_axis] + 1) % drawn.shape[main_axis]] + index_at[main_axis + 1:]
    return drawn.at[tuple(index_at)].set(smallest).at[tuple(neighbour)].set(high)


def shard_levels(rng, dims, cuts, least, high):
    level, own = 1.0, jax.random.fold_in(rng, 6)
    for axis_at, blocks in cuts:
        draws = jnp.exp(jax.random.uniform(jax.random.fold_in(own, axis_at), (blocks,), jnp.float32, least / len(cuts), high / len(cuts)))
        level = level * jnp.repeat(draws, dims[axis_at] // blocks).reshape([-1 if axis == axis_at else 1 for axis in range(len(dims))])
    return level


def normal_values(own_key, dims, scale, most, cuts=(), held_as=jnp.bfloat16):
    drawn = scale * jax.random.normal(own_key, dims, jnp.float32)
    if cuts:
        drawn = drawn * shard_levels(own_key, dims, cuts, -0.22, 0.18)
    return jnp.clip(drawn, -most, most).astype(held_as)


def setup_inputs(seed: int = 0) -> dict:
    seeds = jax.random.split(jax.random.key(seed), 15)
    return {
        "fine_tokens": normal_values(seeds[0], (LEV, NLAT, NLON, D), 1.0, 6.0, ((1, 8), (2, 32))),
        "grad_out": normal_values(seeds[1], (LEV, NLAT, NLON, D), 1.0, 6.0, ((1, 8), (2, 32))),
        "window_class": place_ends(jax.random.randint(seeds[2], (LEV, NLAT, NLON), 0, 3), jax.random.fold_in(seeds[2], 1), 0, 2).astype(jnp.int32),
        "temper_fine": jnp.clip(jnp.exp(jax.random.uniform(seeds[3], (HF,), jnp.float32, math.log(4.0), math.log(20.0))), 4.0, 20.0),
        "temper_coarse": jnp.clip(jnp.exp(jax.random.uniform(seeds[4], (HC,), jnp.float32, math.log(4.0), math.log(20.0))), 4.0, 20.0),
        "gain_fine": jnp.clip(1.0 + 0.18 * jax.random.normal(seeds[5], (D,), jnp.float32), 0.1, 1.9),
        "fine_qkv": normal_values(seeds[6], (D, 3 * D), D ** -0.5, 0.25, ((0, 32),)),
        "fine_out": normal_values(seeds[7], (D, D), D ** -0.5, 0.25, ((0, 32),)),
        "gain_merge": jnp.clip(1.0 + 0.18 * jax.random.normal(seeds[8], (4 * D,), jnp.float32), 0.1, 1.9),
        "merge_weight": normal_values(seeds[9], (4 * D, DC), (4 * D) ** -0.5, 0.125, ((0, 32),)),
        "gain_coarse": jnp.clip(1.0 + 0.18 * jax.random.normal(seeds[10], (DC,), jnp.float32), 0.1, 1.9),
        "coarse_qkv": normal_values(seeds[11], (DC, 3 * DC), DC ** -0.5, 0.1875, ((0, 32),)),
        "coarse_out": normal_values(seeds[12], (DC, DC), DC ** -0.5, 0.1875, ((0, 32),)),
        "split_weight": normal_values(seeds[13], (DC, 4 * D), DC ** -0.5, 0.1875, ((0, 32),)),
    }


LN_EPS = 1e-05
UNIT_EPS = 1e-06

def layer_norm(values, scales):
    average = lax.optimization_barrier(jnp.mean(values, axis=-1, keepdims=True))
    centred = values - average
    spread = lax.optimization_barrier(jnp.mean(centred * centred, axis=-1, keepdims=True))
    return (centred * lax.rsqrt(spread + LN_EPS) * scales).astype(jnp.bfloat16)

def unit_rows(values):
    widened = values.astype(jnp.float32)
    total = lax.optimization_barrier(jnp.sum(widened * widened, axis=-1, keepdims=True))
    return (widened * lax.rsqrt(total + UNIT_EPS)).astype(jnp.bfloat16)

def to_windows(layout, win_rows):
    lev_count, row_count, col_count = (layout.shape[0], layout.shape[1], layout.shape[2])
    trailing = tuple(layout.shape[3:])
    blocks = layout.reshape((lev_count // WL, WL, row_count // win_rows, win_rows, col_count // WLON, WLON) + trailing)
    order_list = (0, 2, 4, 1, 3, 5) + tuple(range(6, 6 + len(trailing)))
    return blocks.transpose(order_list).reshape((-1, WL * win_rows * WLON) + trailing)

def from_windows(blocks, dims_out, win_rows):
    lev_count, row_count, col_count = (dims_out[0], dims_out[1], dims_out[2])
    trailing = tuple(dims_out[3:])
    layout = blocks.reshape((lev_count // WL, row_count // win_rows, col_count // WLON, WL, win_rows, WLON) + trailing)
    order_list = (0, 3, 1, 4, 2, 5) + tuple(range(6, 6 + len(trailing)))
    return layout.transpose(order_list).reshape(tuple(dims_out))

def attend(queries, key_rows, value_rows, temper, allowed):
    scores = jnp.einsum('wnhe,wmhe->whnm', queries.astype(jnp.float32), key_rows.astype(jnp.float32))
    scores = scores * temper[None, :, None, None]
    weights = jnp.exp(scores)
    if allowed is not None:
        weights = jnp.where(allowed[:, None], weights, 0.0)
    chances = (weights / lax.optimization_barrier(jnp.sum(weights, axis=-1, keepdims=True))).astype(jnp.bfloat16)
    mixed = jnp.einsum('whnm,wmhe->wnhe', chances.astype(jnp.float32), value_rows.astype(jnp.float32))
    return mixed.astype(jnp.bfloat16).reshape(mixed.shape[0], mixed.shape[1], -1)

def window_block(layout, labels, qkv_weight, out_weight, temper):
    blocks = to_windows(layout, WLAT)
    win_count, tok_count, feat_count = blocks.shape
    head_count = temper.shape[0]
    head_size = qkv_weight.shape[1] // (3 * head_count)
    qkv_act = jnp.dot(blocks.reshape(-1, feat_count), qkv_weight, preferred_element_type=jnp.float32).astype(jnp.bfloat16)
    qkv_act = qkv_act.reshape(win_count, tok_count, 3, head_count, head_size)
    allowed = None
    if labels is not None:
        marks = to_windows(labels, WLAT)
        allowed = marks[:, :, None] == marks[:, None, :]
    mixed = attend(unit_rows(qkv_act[:, :, 0]), unit_rows(qkv_act[:, :, 1]), qkv_act[:, :, 2], temper, allowed)
    delta = jnp.dot(mixed.reshape(win_count * tok_count, -1), out_weight, preferred_element_type=jnp.float32)
    return from_windows(delta.reshape(win_count, tok_count, -1), tuple(layout.shape[:3]) + (out_weight.shape[1],), WLAT)

def merge_tokens(layout):
    lev_count, row_count, col_count, feat_count = layout.shape
    pieces = layout.reshape(lev_count, row_count // 2, 2, col_count // 2, 2, feat_count)
    pieces = pieces.transpose(0, 1, 3, 4, 2, 5)
    return pieces.reshape(lev_count, row_count // 2, col_count // 2, 4 * feat_count)

def split_tokens(layout, feat_count):
    lev_count, row_count, col_count = (layout.shape[0], layout.shape[1], layout.shape[2])
    pieces = layout.reshape(lev_count, row_count, col_count, 2, 2, feat_count).transpose(0, 1, 4, 2, 3, 5)
    return pieces.reshape(lev_count, 2 * row_count, 2 * col_count, feat_count)

def merge_section(hidden, scales, weight_all):
    merged = merge_tokens(hidden)
    merged_norm = layer_norm(merged.astype(jnp.float32), scales)
    lead_dims = tuple(merged_norm.shape[:3])
    coarse = jnp.dot(merged_norm.reshape(-1, merged_norm.shape[3]), weight_all, preferred_element_type=jnp.float32)
    return coarse.astype(jnp.bfloat16).reshape(lead_dims + (weight_all.shape[1],))

def split_section(coarse_next, weight_all):
    lead_dims = tuple(coarse_next.shape[:3])
    spread_out = jnp.dot(coarse_next.reshape(-1, coarse_next.shape[3]), weight_all, preferred_element_type=jnp.float32)
    return split_tokens(spread_out.reshape(lead_dims + (weight_all.shape[1],)), weight_all.shape[1] // 4)

def forward(fine_tokens, window_class, temper_fine, temper_coarse, gain_fine, fine_qkv, fine_out, gain_merge, merge_weight, gain_coarse, coarse_qkv, coarse_out, split_weight):
    wide_in = fine_tokens.astype(jnp.float32)
    normed = layer_norm(wide_in, gain_fine)
    rolled = jnp.roll(normed, (-SLAT, -SLON), axis=(1, 2))
    row_index = jnp.arange(NLAT)
    pole_mark = (row_index >= NLAT - SLAT).astype(jnp.int32)
    labels = window_class + 3 * pole_mark[None, :, None]
    fine_delta = window_block(rolled, labels, fine_qkv, fine_out, temper_fine)
    fine_delta = jnp.roll(fine_delta, (SLAT, SLON), axis=(1, 2)).astype(jnp.bfloat16)
    hidden = (wide_in + fine_delta.astype(jnp.float32)).astype(jnp.bfloat16)
    coarse = merge_section(hidden, gain_merge, merge_weight)
    coarse_wide = coarse.astype(jnp.float32)
    coarse_norm = layer_norm(coarse_wide, gain_coarse)
    coarse_delta = window_block(coarse_norm, None, coarse_qkv, coarse_out, temper_coarse)
    coarse_next = (coarse_wide + coarse_delta).astype(jnp.bfloat16)
    split_add = split_section(coarse_next, split_weight)
    return (hidden.astype(jnp.float32) + split_add).astype(jnp.bfloat16)

def reference(fine_tokens, grad_out, window_class, temper_fine, temper_coarse, gain_fine, fine_qkv, fine_out, gain_merge, merge_weight, gain_coarse, coarse_qkv, coarse_out, split_weight):

    def apply_all(values):
        return forward(values, window_class, temper_fine, temper_coarse, gain_fine, fine_qkv, fine_out, gain_merge, merge_weight, gain_coarse, coarse_qkv, coarse_out, split_weight)
    output, pull_back = jax.vjp(apply_all, fine_tokens)
    grad_in, = pull_back(grad_out)
    return (output, grad_in)
```

```python
import functools

import jax
import jax.numpy as jnp
import numpy as np
from jax import lax
from jax.experimental import pallas as pl
from jax.experimental.pallas import tpu as pltpu
from jax.sharding import PartitionSpec as P

MESH = pl.DeviceIdType.MESH
F32, BF16 = jnp.float32, jnp.bfloat16
LN_EPS = 1e-05
UNIT_EPS = 1e-06

LEV, ROWS, COLS = 2, 6, 24
NTOK = LEV * ROWS * COLS
NWIN = 144
NMINE = 72
HALO = 208
NCAT = 512
PIECES = ((0, 112), (112, 48), (160, 48))
PAD = 80


def layout_tables():
    flat = np.arange(NTOK).reshape(LEV, ROWS, COLS)
    merged_of = np.zeros(NTOK, np.int64)
    order = np.concatenate([flat[:, di::2, dj::2].reshape(-1) for dj in (0, 1) for di in (0, 1)])
    merged_of[order] = np.arange(NTOK)
    to_merged = np.zeros((NTOK, NTOK), np.float32)
    to_merged[np.arange(NTOK), order] = 1
    halo_slot = {}
    at = {"lat": 0, "lon": 112, "diag": 160}
    send = np.zeros((HALO, NTOK), np.float32)
    for l in range(LEV):
        for i in range(ROWS):
            for j in range(COLS):
                kind = {(1, 0): "lat", (0, 1): "lon", (1, 1): "diag"}.get((int(i < 3), int(j < 6)))
                if kind:
                    halo_slot[l, i, j] = at[kind]
                    send[at[kind], merged_of[flat[l, i, j]]] = 1
                    at[kind] += 1
    region = np.zeros((NTOK, NCAT), np.float32)
    row = 0
    for w in range(2):
        for l in range(LEV):
            for i in range(ROWS):
                for j in range(12):
                    si, sj = i + 3, 12 * w + j + 6
                    if si < ROWS and sj < COLS:
                        region[row, merged_of[flat[l, si, sj]]] = 1
                    else:
                        region[row, NTOK + halo_slot[l, si % ROWS, sj % COLS]] = 1
                    row += 1
    own, halo = region[:, :NTOK], region[:, NTOK:NTOK + HALO]
    back = np.zeros((NTOK, NCAT), np.float32)
    back[:, :NTOK] = own.T
    back[:, NTOK:NTOK + HALO] = send.T
    tables = (to_merged, to_merged.T, send, region, back, halo.T)
    return [np.ascontiguousarray(t).astype(jnp.bfloat16) for t in tables]


def dot(a, b, dims=((1,), (0,))):
    return lax.dot_general(a, b, (dims, ((), ())), preferred_element_type=F32)


TRANS_B = ((1,), (1,))
TRANS_A = ((0,), (0,))


def normalise(values):
    average = jnp.mean(values, axis=-1, keepdims=True)
    centred = values - average
    scale = lax.rsqrt(jnp.mean(centred * centred, axis=-1, keepdims=True) + LN_EPS)
    return centred * scale, scale


def norm_back(grad, gains, unit, scale):
    grad = grad * gains
    part = jnp.mean(grad, axis=-1, keepdims=True)
    along = jnp.mean(grad * unit, axis=-1, keepdims=True)
    return scale * (grad - part - unit * along)


def half_mask(rows):
    return lax.broadcasted_iota(jnp.int32, (rows, 128), 1) < 64


def half_sums(values, low):
    first = jnp.sum(jnp.where(low, values, 0.0), axis=-1, keepdims=True)
    second = jnp.sum(jnp.where(low, 0.0, values), axis=-1, keepdims=True)
    return jnp.where(low, first, second)


def attend_forward(act, mixed, chances, rows, first, temper, temper_at, allowed):
    low = half_mask(NWIN)

    def pair(p, carry):
        q = act[rows, pl.ds(pl.multiple_of(p * 128, 128), 128)].astype(F32)
        k = act[rows, pl.ds(pl.multiple_of(p * 128 + 512, 128), 128)].astype(F32)
        v = act[rows, pl.ds(pl.multiple_of(p * 128 + 1024, 128), 128)]
        q = q * lax.rsqrt(half_sums(q * q, low) + UNIT_EPS)
        k = (k * lax.rsqrt(half_sums(k * k, low) + UNIT_EPS)).astype(BF16)
        mixes = []
        for j in range(2):
            mine = low if j == 0 else jnp.logical_not(low)
            scores = dot(jnp.where(mine, q, 0.0).astype(BF16), k, TRANS_B) * temper[temper_at + 2 * p + j]
            weights = jnp.exp(scores)
            if allowed is not None:
                weights = weights * allowed
            chance = weights * (1.0 / jnp.sum(weights, axis=-1, keepdims=True))
            chances[first + 2 * p + j] = chance
            mixes.append(dot(chance.astype(BF16), v))
        mixed[rows, pl.ds(pl.multiple_of(p * 128, 128), 128)] = jnp.where(low, mixes[0], mixes[1]).astype(BF16)
        return carry

    lax.fori_loop(0, 4, pair, 0)


def attend_backward(act, grad_mixed, grad_act, chances, rows, first, temper, temper_at):
    low = half_mask(NWIN)

    def pair(p, carry):
        at = [pl.ds(pl.multiple_of(p * 128 + 512 * t, 128), 128) for t in range(3)]
        q, k, v = (act[rows, s].astype(F32) for s in at)
        q_scale = lax.rsqrt(half_sums(q * q, low) + UNIT_EPS)
        k_scale = lax.rsqrt(half_sums(k * k, low) + UNIT_EPS)
        q, k = q * q_scale, k * k_scale
        q_low, k_low = q.astype(BF16), k.astype(BF16)
        grad = grad_mixed[rows, at[0]]
        gq, gk, gv = [], [], []
        for j in range(2):
            mine = low if j == 0 else jnp.logical_not(low)
            chance = chances[first + 2 * p + j]
            gc = dot(grad, jnp.where(mine, v, 0.0).astype(BF16), TRANS_B)
            gc = chance * (gc - jnp.sum(gc * chance, axis=-1, keepdims=True))
            gs = (gc * temper[temper_at + 2 * p + j]).astype(BF16)
            gq.append(dot(gs, k_low))
            gk.append(dot(gs, q_low, TRANS_A))
            gv.append(dot(chance.astype(BF16), grad, TRANS_A))
        gq, gk, gv = (jnp.where(low, *parts) for parts in (gq, gk, gv))
        grad_act[rows, at[0]] = (q_scale * (gq - q * half_sums(gq * q, low))).astype(BF16)
        grad_act[rows, at[1]] = (k_scale * (gk - k * half_sums(gk * k, low))).astype(BF16)
        grad_act[rows, at[2]] = gv.astype(BF16)
        return carry

    lax.fori_loop(0, 4, pair, 0)


WEIGHTS = (
    ("fq", 16, 1536, True),
    ("fo", 16, 512, False),
    ("mw", 64, 1024, True),
    ("cq", 32, 1536, False),
    ("co", 32, 1024, False),
    ("sp", 32, 2048, True),
)
SEMS_PER_WEIGHT = 30


def kernel(
    x_ref, g_ref, marks_ref, temper_fine, temper_coarse, gain_fine, gain_merge, gain_coarse,
    fq_in, fo_in, mw_in, cq_in, co_in, sp_in,
    to_merged, from_merged, send_table, region_table, back_table, halo_table,
    out_ref, gin_ref,
    fq, fo, mw, cq, co, sp,
    buf0, buf1, buf2, buf3, sbuf0, sbuf1, sbuf2, sbuf3,
    prx, pry, prz, prw, psx, psy, psz, psw,
    xm_ref, act, mixed, gact, chances, hid, cact, cmixed, cchances, coarse_ref, cnext_ref, gnext_ref, mn_ref, wide_ref, gh_ref,
    sems, halo_sems, pair_sems,
):
    lat, lon = lax.axis_index("lat"), lax.axis_index("lon")
    y, x_lo = lat // 2, lat % 2
    z, x_hi, core = lon // 4, (lon // 2) % 2, lon % 2

    def at_lat(by):
        return lax.rem(lat + 8 + by, 8)

    def at_lon(by):
        return lax.rem(lon + 32 + by, 32)

    z_next, z_prev = (lat, at_lon(4)), (lat, at_lon(-4))
    y_next, y_prev = (at_lat(2), lon), (at_lat(-2), lon)
    x_mate = (lat + 1 - 2 * x_lo, lon + 2 - 4 * x_hi)
    sibling = (lat, lon + 1 - 2 * core)
    pair_mate = (lat + 1 - 2 * x_lo, lon)
    behind = ((at_lat(-1), lon), (lat, at_lon(-1)), (at_lat(-1), at_lon(-1)))
    ahead = ((at_lat(1), lon), (lat, at_lon(1)), (at_lat(1), at_lon(1)))
    friends = (z_next, z_prev, y_next, y_prev, x_mate) + behind + ahead

    unfinished = []

    def send(src, dst, sem_out, sem_in, device):
        copy = pltpu.make_async_remote_copy(
            src_ref=src, dst_ref=dst, send_sem=sem_out, recv_sem=sem_in, device_id=device, device_id_type=MESH
        )
        copy.start()
        return copy

    def arrived(dst, sem_out, sem_in, device):
        pltpu.make_async_remote_copy(
            src_ref=dst, dst_ref=dst, send_sem=sem_out, recv_sem=sem_in, device_id=device, device_id_type=MESH
        ).wait_recv()

    inputs = {"fq": fq_in, "fo": fo_in, "mw": mw_in, "cq": cq_in, "co": co_in, "sp": sp_in}
    buffers = {"fq": fq, "fo": fo, "mw": mw, "cq": cq, "co": co, "sp": sp}

    def weight_events(index):
        name, rows, cols, last_y = WEIGHTS[index]
        src, whole = inputs[name], buffers[name]
        width = cols // 4 if last_y else cols
        if last_y:
            columns = pl.ds(pl.multiple_of(y * width, 128), width)
        else:
            columns = slice(None)
        sem = [sems.at[index, i] for i in range(SEMS_PER_WEIGHT)]

        def block(zz):
            return whole.at[zz, :, core, :, columns]

        def stage_local():
            if name == "cq":
                for t in range(3):
                    from_at = pl.ds(pl.multiple_of(t * 1024 + x_lo * 512, 128), 512)
                    pltpu.make_async_copy(
                        src.at[:, from_at], whole.at[z, x_hi, core, :, pl.ds(t * 512, 512)], sem[t]
                    ).start()
            else:
                pltpu.make_async_copy(src.at[:, columns], whole.at[z, x_hi, core, :, columns], sem[0]).start()

        def stage_swap():
            if name == "cq":
                for t in range(3):
                    from_at = pl.ds(pl.multiple_of(t * 1024 + (1 - x_lo) * 512, 128), 512)
                    unfinished.append(send(
                        src.at[:, from_at], whole.at[z, x_hi, core, :, pl.ds(t * 512, 512)], sem[3 + t], sem[6 + t], x_mate
                    ))
            else:
                unfinished.append(send(
                    src.at[:, columns], whole.at[z, x_hi, core, :, columns], sem[3], sem[6], x_mate
                ))

        def forward(step):
            zz = lax.rem(z + 8 - step, 8)
            if step < 4:
                unfinished.append(send(block(zz), block(zz), sem[9 + step], sem[13 + step], z_next))

        def backward(step):
            zz = lax.rem(z + step, 8)
            if step < 3:
                unfinished.append(send(block(zz), block(zz), sem[17 + step], sem[20 + step], z_prev))

        def to_core(ref):
            send(ref, ref, sem[23], sem[24], sibling)

        def first():
            if name == "cq":
                for t in range(3):
                    part = whole.at[z, x_hi, core, :, pl.ds(t * 512, 512)]
                    pltpu.make_async_copy(part, part, sem[t]).wait()
                    arrived(whole.at[z, 1 - x_hi, core, :, pl.ds(t * 512, 512)], sem[3 + t], sem[6 + t], x_mate)
            else:
                part = whole.at[z, x_hi, core, :, columns]
                pltpu.make_async_copy(part, part, sem[0]).wait()
                arrived(whole.at[z, 1 - x_hi, core, :, columns], sem[3], sem[6], x_mate)
            forward(0)
            backward(0)
            if not last_y:
                to_core(block(z))

        def ring(step):
            zz = lax.rem(z + 8 - step, 8)
            arrived(block(zz), sem[9 + step - 1], sem[13 + step - 1], z_next)
            forward(step)
            if not last_y:
                to_core(block(zz))
            if step < 4:
                zz = lax.rem(z + step, 8)
                arrived(block(zz), sem[17 + step - 1], sem[20 + step - 1], z_prev)
                backward(step)
                if not last_y:
                    to_core(block(zz))

        def quarter(by, half=None):
            yy = lax.rem(y + 4 + by, 4)
            where = pl.ds(pl.multiple_of(yy * width, 128), width)
            if half is None:
                return whole.at[:, :, core, :, where]
            return whole.at[pl.ds(4 * half, 4), :, core, :, where]

        def along_y():
            unfinished.append(send(quarter(0), quarter(0), sem[25], sem[26], y_next))
            unfinished.append(send(quarter(0), quarter(0), sem[27], sem[28], y_prev))
            to_core(quarter(0))

        def along_y_second():
            arrived(quarter(-1), sem[25], sem[26], y_next)
            unfinished.append(send(quarter(-1, 0), quarter(-1, 0), sem[29], sem[5], y_next))
            to_core(quarter(-1))
            arrived(quarter(1), sem[27], sem[28], y_prev)
            unfinished.append(send(quarter(1, 1), quarter(1, 1), sem[7], sem[8], y_prev))
            to_core(quarter(1))

        def along_y_third():
            arrived(quarter(2, 0), sem[29], sem[5], y_next)
            arrived(quarter(2, 1), sem[7], sem[8], y_prev)
            to_core(quarter(2))

        def ready():
            arrived(whole.at[:, :, 1 - core], sem[23], sem[24], sibling)

        def sent():
            pltpu.make_async_remote_copy(
                src_ref=whole.at[:, :, core], dst_ref=whole.at[:, :, core], send_sem=sem[23], recv_sem=sem[24],
                device_id=sibling, device_id_type=MESH,
            ).wait_send()

        steps = [first] + [functools.partial(ring, s) for s in range(1, 5)]
        if last_y:
            steps += [along_y, along_y_second, along_y_third]
        return {"local": stage_local, "swap": stage_swap, "steps": steps, "ready": ready, "sent": sent}

    events = [weight_events(i) for i in range(6)]
    place = {spec[0]: i for i, spec in enumerate(WEIGHTS)}
    done = [0] * 6

    def advance(name, count=1):
        index = place[name]
        for _ in range(count):
            if done[index] < len(events[index]["steps"]):
                events[index]["steps"][done[index]]()
                done[index] += 1

    def finish(name):
        advance(name, 8)
        events[place[name]]["ready"]()

    def halo_send(number, table, rows_from, buffer, staging, devices):
        staging[...] = dot(table[...], rows_from).astype(BF16)
        for i, (at, count) in enumerate(PIECES):
            unfinished.append(send(
                staging.at[pl.ds(at, count)], buffer.at[pl.ds(NTOK + at, count)],
                halo_sems.at[number, i], halo_sems.at[number, 3 + i], devices[i],
            ))

    def halo_wait(number, buffer, devices):
        for i, (at, count) in enumerate(PIECES):
            arrived(buffer.at[pl.ds(NTOK + at, count)], halo_sems.at[number, i], halo_sems.at[number, 3 + i], devices[i])

    def pair_send(number, values, staging, buffer):
        staging[...] = jnp.concatenate([values, jnp.zeros((PAD - NMINE, values.shape[1]), F32)], axis=0).astype(BF16)
        unfinished.append(send(staging, buffer, pair_sems.at[number, 0], pair_sems.at[number, 1], pair_mate))

    def pair_wait(number, buffer):
        arrived(buffer, pair_sems.at[number, 0], pair_sems.at[number, 1], pair_mate)
        return buffer[...].astype(F32)[:NMINE]

    for event in events:
        event["local"]()
    barrier = pltpu.get_barrier_semaphore()
    for friend in friends:
        pl.semaphore_signal(barrier, inc=1, device_id=friend, device_id_type=MESH)
    xm = dot(to_merged[...], x_ref[...]).astype(BF16)
    xm_ref[...] = xm
    for buffer in (buf0, buf1, buf2, buf3):
        buffer[pl.ds(NTOK + HALO, NCAT - NTOK - HALO), :] = jnp.zeros((NCAT - NTOK - HALO, 512), BF16)
    buf0[pl.ds(0, NTOK), :] = xm
    pl.semaphore_wait(barrier, len(friends))
    for event in events[:2]:
        event["swap"]()
    halo_send(0, send_table, xm, buf0, sbuf0, behind)
    for event in events[2:]:
        event["swap"]()
    for _ in range(3):
        advance("fq")
        advance("fo")
    gm = dot(to_merged[...], g_ref[...]).astype(BF16)
    allowed = [dot(marks_ref[w], marks_ref[w], TRANS_B) for w in range(2)]
    advance("fq")
    advance("fo")
    halo_wait(0, buf0, behind)
    region = dot(region_table[...], buf0[...])
    unit, _ = normalise(region)
    region = (unit * gain_fine[...]).astype(BF16)
    advance("fq")
    advance("fo")
    advance("mw")
    advance("cq")
    advance("fq")
    advance("mw")
    advance("fq")
    advance("mw")
    advance("fq")
    finish("fq")

    def all_rows(ref, columns):
        value = ref[:, :, :, :, columns]
        return value.reshape(-1, value.shape[-1])

    for t in range(3):
        part = pl.ds(t * 512, 512)
        act[:, part] = dot(region, all_rows(fq, part)).astype(BF16)
    advance("cq")
    for w in range(2):
        attend_forward(act, mixed, chances, pl.ds(w * NWIN, NWIN), 8 * w, temper_fine, 0, allowed[w])
        advance("mw")
        advance("cq")
    finish("fo")
    delta = dot(mixed[...], all_rows(fo, slice(None))).astype(BF16)
    buf1[pl.ds(0, NTOK), :] = delta
    halo_send(1, halo_table, delta, buf1, sbuf1, ahead)
    advance("mw")
    advance("cq")
    advance("co")
    halo_wait(1, buf1, ahead)
    hidden = (xm_ref[...].astype(F32) + dot(back_table[...], buf1[...])).astype(BF16)
    hid[...] = hidden

    def cells(values):
        return jnp.concatenate([values[NMINE * i:NMINE * (i + 1)] for i in range(4)], axis=1)

    unit, merge_scale = normalise(cells(hidden.astype(F32)))
    wide_ref[...] = unit
    mn_ref[...] = (unit * gain_merge[...]).astype(BF16)
    finish("mw")

    def merge_step(n, carry):
        part = pl.ds(pl.multiple_of(n * 256, 256), 256)
        coarse_ref[:, part] = dot(mn_ref[...], all_rows(mw, part)).astype(BF16).astype(F32)
        return carry

    lax.fori_loop(0, 4, merge_step, 0)
    coarse = coarse_ref[...]
    coarse_unit, coarse_scale = normalise(coarse)
    coarse_norm = (coarse_unit * gain_coarse[...]).astype(BF16).astype(F32)
    pair_send(0, coarse_norm, psx, prx)
    advance("cq")
    advance("co")
    advance("sp")

    grad_cells = cells(gm.astype(F32)).astype(BF16)
    window = jnp.concatenate([coarse_norm, pair_wait(0, prx)], axis=0).astype(BF16)
    finish("cq")

    for t in range(3):
        part = pl.ds(t * 512, 512)
        cact[:, part] = dot(window, all_rows(cq, part)).astype(BF16)
    advance("co")
    advance("sp")
    attend_forward(cact, cmixed, cchances, pl.ds(0, NWIN), 0, temper_coarse, 8 * x_lo, None)
    advance("co")
    advance("sp")
    finish("co")
    co_mine = co[pl.ds(4 * x_lo, 4)].reshape(512, 1024)
    partial = dot(cmixed[...], co_mine)
    pair_send(1, partial[NMINE:], psy, pry)
    finish("sp")

    def grad_step(n, carry):
        rows = sp[pl.ds(2 * n, 2)].reshape(256, 2048)
        gnext_ref[:, pl.ds(pl.multiple_of(n * 256, 256), 256)] = dot(grad_cells, rows, TRANS_B).astype(BF16).astype(F32)
        return carry

    lax.fori_loop(0, 4, grad_step, 0)
    grad_next = gnext_ref[...]
    pair_send(2, grad_next, psz, prz)
    coarse_next = (coarse + (partial[:NMINE] + pair_wait(1, pry))).astype(BF16)
    cnext_ref[...] = coarse_next

    for q in range(4):
        part = pl.ds(q * 512, 512)
        rows = pl.ds(q * NMINE, NMINE)
        wide_part = dot(cnext_ref[...], all_rows(sp, part))
        gh_ref[rows, :] = hid[rows, :].astype(F32) + wide_part
    out_ref[...] = dot(from_merged[...], gh_ref[...].astype(BF16)).astype(BF16)

    grad_window = jnp.concatenate([grad_next, pair_wait(2, prz)], axis=0).astype(BF16)
    mixed[pl.ds(0, NWIN), :] = dot(grad_window, co_mine, TRANS_B).astype(BF16)
    attend_backward(cact, mixed, gact, cchances, pl.ds(0, NWIN), 0, temper_coarse, 8 * x_lo)
    grad_act = gact[pl.ds(0, NWIN), :]
    partial = jnp.concatenate(
        [dot(grad_act, cq[pl.ds(2 * n, 2)].reshape(256, 1536), TRANS_B) for n in range(4)], axis=1
    )
    pair_send(3, partial[NMINE:], psw, prw)
    grad_norm = (partial[:NMINE] + pair_wait(3, prw)).astype(BF16).astype(F32)
    grad_coarse = (grad_next + norm_back(grad_norm, gain_coarse[...], coarse_unit, coarse_scale)).astype(BF16)
    grad_merged = jnp.concatenate(
        [dot(grad_coarse, mw[n].reshape(256, 1024), TRANS_B) for n in range(8)], axis=1
    ).astype(BF16).astype(F32)
    grad_merged = norm_back(grad_merged, gain_merge[...], wide_ref[...], merge_scale).astype(BF16).astype(F32)
    for q in range(4):
        rows = pl.ds(q * NMINE, NMINE)
        gh_ref[rows, :] = grad_merged[:, q * 512:(q + 1) * 512]
    grad_hidden = (gm.astype(F32) + gh_ref[...]).astype(BF16)
    hid[...] = grad_hidden

    buf2[pl.ds(0, NTOK), :] = grad_hidden
    halo_send(2, send_table, grad_hidden, buf2, sbuf2, behind)
    halo_wait(2, buf2, behind)
    grad_region = dot(region_table[...], buf2[...]).astype(BF16)
    mixed[...] = dot(grad_region, all_rows(fo, slice(None)), TRANS_B).astype(BF16)
    for w in range(2):
        attend_backward(act, mixed, gact, chances, pl.ds(w * NWIN, NWIN), 8 * w, temper_fine, 0)
    grad_region = dot(gact[...], all_rows(fq, slice(None)), TRANS_B).astype(BF16)
    buf3[pl.ds(0, NTOK), :] = grad_region
    halo_send(3, halo_table, grad_region, buf3, sbuf3, ahead)
    unit, scale = normalise(xm_ref[...].astype(F32))
    halo_wait(3, buf3, ahead)
    grad_norm = dot(back_table[...], buf3[...]).astype(BF16).astype(F32)
    grad_in = hid[...].astype(F32) + norm_back(grad_norm, gain_fine[...], unit, scale)
    gin_ref[...] = dot(from_merged[...], grad_in.astype(BF16)).astype(BF16)

    for copy in unfinished:
        copy.wait_send()
    for event in events:
        event["sent"]()


def per_device(
    fine_tokens, grad_out, window_class, temper_fine, temper_coarse, gain_fine, fine_qkv, fine_out, gain_merge,
    merge_weight, gain_coarse, coarse_qkv, coarse_out, split_weight,
):
    at_pole = (lax.axis_index("lat") == lax.axis_size("lat") - 1) & (jnp.arange(ROWS) >= 3)
    labels = window_class + 3 * at_pole.astype(jnp.int32)[None, :, None]
    labels = labels.reshape(LEV, ROWS, 2, 12).transpose(2, 0, 1, 3).reshape(2, NWIN)
    marks = (labels[:, :, None] == jnp.arange(128)[None, None, :]).astype(BF16)
    vmem = pl.BlockSpec(memory_space=pltpu.VMEM)
    smem = pl.BlockSpec(memory_space=pltpu.SMEM)
    anyplace = pl.BlockSpec(memory_space=pl.ANY)
    scratch = [pltpu.VMEM((8, 2, 2, rows, cols), BF16) for _, rows, cols, _ in WEIGHTS]
    scratch += [pltpu.VMEM((NCAT, 512), BF16)] * 4 + [pltpu.VMEM((HALO, 512), BF16)] * 4
    scratch += [pltpu.VMEM((PAD, 1024), BF16)] * 8
    scratch += [
        pltpu.VMEM((NTOK, 512), BF16),
        pltpu.VMEM((NTOK, 1536), BF16),
        pltpu.VMEM((NTOK, 512), BF16),
        pltpu.VMEM((NTOK, 1536), BF16),
        pltpu.VMEM((16, NWIN, NWIN), F32),
        pltpu.VMEM((NTOK, 512), BF16),
        pltpu.VMEM((NWIN, 1536), BF16),
        pltpu.VMEM((NWIN, 512), BF16),
        pltpu.VMEM((8, NWIN, NWIN), F32),
        pltpu.VMEM((NMINE, 1024), F32),
        pltpu.VMEM((NMINE, 1024), BF16),
        pltpu.VMEM((NMINE, 1024), F32),
        pltpu.VMEM((NMINE, 2048), BF16),
        pltpu.VMEM((NMINE, 2048), F32),
        pltpu.VMEM((NTOK, 512), F32),
        pltpu.SemaphoreType.DMA((6, SEMS_PER_WEIGHT)),
        pltpu.SemaphoreType.DMA((4, 6)),
        pltpu.SemaphoreType.DMA((4, 2)),
    ]
    tables = layout_tables()
    output, grad_in = pl.pallas_call(
        kernel,
        out_shape=[jax.ShapeDtypeStruct((NTOK, 512), BF16)] * 2,
        in_specs=[vmem] * 3 + [smem] * 2 + [vmem] * 3 + [anyplace] * 6 + [vmem] * 6,
        out_specs=[vmem] * 2,
        scratch_shapes=scratch,
        compiler_params=pltpu.CompilerParams(
            collective_id=0, has_side_effects=True, vmem_limit_bytes=56 * 1024 * 1024
        ),
    )(
        fine_tokens.reshape(NTOK, 512), grad_out.reshape(NTOK, 512), marks, temper_fine, temper_coarse,
        gain_fine.reshape(1, -1), gain_merge.reshape(1, -1), gain_coarse.reshape(1, -1),
        fine_qkv, fine_out, merge_weight, coarse_qkv, coarse_out, split_weight, *tables,
    )
    return output.reshape(fine_tokens.shape), grad_in.reshape(fine_tokens.shape)


def solution(mesh):
    tiles = P(None, "lat", "lon", None)
    shards = P("lon", None)
    return jax.shard_map(
        per_device,
        mesh=mesh,
        in_specs=(
            tiles, tiles, P(None, "lat", "lon"), P(), P(), P(), shards, shards, P(), shards, P(), shards, shards, shards,
        ),
        out_specs=(tiles, tiles),
        check_vma=False,
    )
```

```python
import functools

import jax
import jax.numpy as jnp
import numpy as np
from jax import lax
from jax.experimental import pallas as pl
from jax.experimental.pallas import tpu as pltpu
from jax.sharding import PartitionSpec as P

MESH = pl.DeviceIdType.MESH
F32, BF16 = jnp.float32, jnp.bfloat16
LN_EPS = 1e-05
UNIT_EPS = 1e-06

LEV, ROWS, COLS = 2, 6, 24
NTOK = LEV * ROWS * COLS
NWIN = 144
NMINE = 72
HALO = 208
NCAT = 512
PIECES = ((0, 112), (112, 48), (160, 48))
PAD = 80


def layout_tables():
    flat = np.arange(NTOK).reshape(LEV, ROWS, COLS)
    merged_of = np.zeros(NTOK, np.int64)
    order = np.concatenate([flat[:, di::2, dj::2].reshape(-1) for dj in (0, 1) for di in (0, 1)])
    merged_of[order] = np.arange(NTOK)
    to_merged = np.zeros((NTOK, NTOK), np.float32)
    to_merged[np.arange(NTOK), order] = 1
    halo_slot = {}
    at = {"lat": 0, "lon": 112, "diag": 160}
    send = np.zeros((HALO, NTOK), np.float32)
    for l in range(LEV):
        for i in range(ROWS):
            for j in range(COLS):
                kind = {(1, 0): "lat", (0, 1): "lon", (1, 1): "diag"}.get((int(i < 3), int(j < 6)))
                if kind:
                    halo_slot[l, i, j] = at[kind]
                    send[at[kind], merged_of[flat[l, i, j]]] = 1
                    at[kind] += 1
    region = np.zeros((NTOK, NCAT), np.float32)
    row = 0
    for w in range(2):
        for l in range(LEV):
            for i in range(ROWS):
                for j in range(12):
                    si, sj = i + 3, 12 * w + j + 6
                    if si < ROWS and sj < COLS:
                        region[row, merged_of[flat[l, si, sj]]] = 1
                    else:
                        region[row, NTOK + halo_slot[l, si % ROWS, sj % COLS]] = 1
                    row += 1
    own, halo = region[:, :NTOK], region[:, NTOK:NTOK + HALO]
    back = np.zeros((NTOK, NCAT), np.float32)
    back[:, :NTOK] = own.T
    back[:, NTOK:NTOK + HALO] = send.T
    tables = (to_merged, to_merged.T, send, region, back, halo.T)
    return [np.ascontiguousarray(t).astype(jnp.bfloat16) for t in tables]


def dot(a, b, dims=((1,), (0,))):
    return lax.dot_general(a, b, (dims, ((), ())), preferred_element_type=F32)


TRANS_B = ((1,), (1,))
TRANS_A = ((0,), (0,))


def normalise(values):
    average = jnp.mean(values, axis=-1, keepdims=True)
    centred = values - average
    scale = lax.rsqrt(jnp.mean(centred * centred, axis=-1, keepdims=True) + LN_EPS)
    return centred * scale, scale


def norm_back(grad, gains, unit, scale):
    grad = grad * gains
    part = jnp.mean(grad, axis=-1, keepdims=True)
    along = jnp.mean(grad * unit, axis=-1, keepdims=True)
    return scale * (grad - part - unit * along)


def half_mask(rows):
    return lax.broadcasted_iota(jnp.int32, (rows, 128), 1) < 64


def half_sums(values, low):
    first = jnp.sum(jnp.where(low, values, 0.0), axis=-1, keepdims=True)
    second = jnp.sum(jnp.where(low, 0.0, values), axis=-1, keepdims=True)
    return jnp.where(low, first, second)


def head_columns(p, heads):
    first, step, kind = heads
    return [pl.ds(pl.multiple_of(first + p * step + t * kind, 128), 128) for t in range(3)]


def attend_forward(act, mixed, chances, rows, first, temper, temper_at, allowed, heads, start, stop):
    low = half_mask(NWIN)

    def pair(p, carry):
        q, k, v = (act[rows, s] for s in head_columns(p, heads))
        q, k = q.astype(F32), k.astype(F32)
        q = q * lax.rsqrt(half_sums(q * q, low) + UNIT_EPS)
        k = (k * lax.rsqrt(half_sums(k * k, low) + UNIT_EPS)).astype(BF16)
        mixes = []
        for j in range(2):
            mine = low if j == 0 else jnp.logical_not(low)
            scores = dot(jnp.where(mine, q, 0.0).astype(BF16), k, TRANS_B) * temper[temper_at + 2 * p + j]
            weights = jnp.exp(scores)
            if allowed is not None:
                weights = weights * allowed
            chance = weights * (1.0 / jnp.sum(weights, axis=-1, keepdims=True))
            chances[first + 2 * p + j] = chance
            mixes.append(dot(chance.astype(BF16), v))
        mixed[rows, pl.ds(pl.multiple_of(p * 128, 128), 128)] = jnp.where(low, mixes[0], mixes[1]).astype(BF16)
        return carry

    lax.fori_loop(start, stop, pair, 0)


def attend_backward(act, grad_mixed, grad_act, chances, rows, first, temper, temper_at, heads):
    low = half_mask(NWIN)

    def pair(p, carry):
        at = head_columns(p, heads)
        q, k, v = (act[rows, s].astype(F32) for s in at)
        q_scale = lax.rsqrt(half_sums(q * q, low) + UNIT_EPS)
        k_scale = lax.rsqrt(half_sums(k * k, low) + UNIT_EPS)
        q, k = q * q_scale, k * k_scale
        q_low, k_low = q.astype(BF16), k.astype(BF16)
        grad = grad_mixed[rows, pl.ds(pl.multiple_of(p * 128, 128), 128)]
        gq, gk, gv = [], [], []
        for j in range(2):
            mine = low if j == 0 else jnp.logical_not(low)
            chance = chances[first + 2 * p + j]
            gc = dot(grad, jnp.where(mine, v, 0.0).astype(BF16), TRANS_B)
            gc = chance * (gc - jnp.sum(gc * chance, axis=-1, keepdims=True))
            gs = (gc * temper[temper_at + 2 * p + j]).astype(BF16)
            gq.append(dot(gs, k_low))
            gk.append(dot(gs, q_low, TRANS_A))
            gv.append(dot(chance.astype(BF16), grad, TRANS_A))
        gq, gk, gv = (jnp.where(low, *parts) for parts in (gq, gk, gv))
        grad_act[rows, at[0]] = (q_scale * (gq - q * half_sums(gq * q, low))).astype(BF16)
        grad_act[rows, at[1]] = (k_scale * (gk - k * half_sums(gk * k, low))).astype(BF16)
        grad_act[rows, at[2]] = gv.astype(BF16)
        return carry

    lax.fori_loop(0, 4, pair, 0)


WEIGHTS = (
    ("fk", 16, 512, "x", 512),
    ("fo", 16, 512, "x", 0),
    ("fq", 16, 512, "y", 0),
    ("fv", 16, 512, "y", 1024),
    ("mwa", 64, 512, "x", 0),
    ("mwb", 64, 512, "y", 512),
    ("cq", 32, 1536, "z", None),
    ("co", 32, 1024, "x", 0),
    ("spa", 32, 1024, "x", 0),
    ("spb", 32, 1024, "y", 1024),
)
FINE = ("fk", "fo", "fq", "fv")
SEMS_PER_WEIGHT = 33


def kernel(
    x_ref, g_ref, marks_ref, temper_fine, temper_coarse, gain_fine, gain_merge, gain_coarse,
    fq_in, fo_in, mw_in, cq_in, co_in, sp_in,
    to_merged, from_merged, send_table, region_table, back_table, halo_table,
    out_ref, gin_ref,
    fk, fo, fq, fv, mwa, mwb, cq, co, spa, spb,
    buf0, buf1, buf2, buf3, sbuf0, sbuf1, sbuf2, sbuf3,
    prx, pry, prz, prw, psx, psy, psz, psw,
    xm_ref, act, mixed, gact, chances, hid, cact, cmixed, cchances, coarse_ref, cnext_ref, gnext_ref, mn_ref, wide_ref, gh_ref,
    sems, halo_sems, pair_sems,
):
    lat, lon = lax.axis_index("lat"), lax.axis_index("lon")
    y, x_lo = lat // 2, lat % 2
    z, x_hi, core = lon // 4, (lon // 2) % 2, lon % 2

    def at_lat(by):
        return lax.rem(lat + 8 + by, 8)

    def at_lon(by):
        return lax.rem(lon + 32 + by, 32)

    z_next, z_prev = (lat, at_lon(4)), (lat, at_lon(-4))
    y_next, y_prev = (at_lat(2), lon), (at_lat(-2), lon)
    x = 2 * x_hi + x_lo

    def at_x(by):
        there = lax.rem(x + 4 + by, 4)
        return (2 * y + lax.rem(there, 2), 4 * z + 2 * (there // 2) + core)

    x_next, x_prev = at_x(1), at_x(-1)
    x_mate = (lat + 1 - 2 * x_lo, lon + 2 - 4 * x_hi)
    sibling = (lat, lon + 1 - 2 * core)
    pair_mate = (lat + 1 - 2 * x_lo, lon)
    behind = ((at_lat(-1), lon), (lat, at_lon(-1)), (at_lat(-1), at_lon(-1)))
    ahead = ((at_lat(1), lon), (lat, at_lon(1)), (at_lat(1), at_lon(1)))
    z_all = tuple((lat, at_lon(4 * by)) for by in range(1, 8))
    friends = z_all + (y_next, y_prev, x_next, x_prev, x_mate) + behind + ahead

    unfinished = []

    def send(src, dst, sem_out, sem_in, device):
        copy = pltpu.make_async_remote_copy(
            src_ref=src, dst_ref=dst, send_sem=sem_out, recv_sem=sem_in, device_id=device, device_id_type=MESH
        )
        copy.start()
        return copy

    def arrived(dst, sem_out, sem_in, device):
        pltpu.make_async_remote_copy(
            src_ref=dst, dst_ref=dst, send_sem=sem_out, recv_sem=sem_in, device_id=device, device_id_type=MESH
        ).wait_recv()

    inputs = (fq_in, fo_in, fq_in, fq_in, mw_in, mw_in, cq_in, co_in, sp_in, sp_in)
    buffers = (fk, fo, fq, fv, mwa, mwb, cq, co, spa, spb)

    def weight_events(index):
        name, rows, cols, axis, base = WEIGHTS[index]
        src, whole = inputs[index], buffers[index]
        by_x, by_z = axis == "x", axis == "z"
        width = {"x": cols // 2, "y": cols // 4, "z": cols}[axis]
        at, after, before = (x, x_next, x_prev) if by_x else (y, y_next, y_prev)
        sem = [sems.at[index, i] for i in range(SEMS_PER_WEIGHT)]

        def lanes(part):
            return pl.ds(pl.multiple_of(part * width, 128), width)

        def piece(by, levels):
            there = lax.rem(at + 4 + by, 4)
            if by_z:
                return whole.at[levels, :, core]
            if by_x:
                return whole.at[levels, there // 2, core, :, lanes(lax.rem(there, 2))]
            return whole.at[levels, :, core, :, lanes(there)]

        def block(zz):
            return piece(0, zz)

        def source(parity):
            if by_z:
                return [
                    (pl.ds(pl.multiple_of(t * 1024 + parity * 512, 128), 512), pl.ds(t * 512, 512)) for t in range(3)
                ]
            part = x_lo if by_x else y
            return [(pl.ds(pl.multiple_of(base + part * width, 128), width), lanes(part))]

        def stage_local():
            for t, (from_at, to_at) in enumerate(source(x_lo)):
                pltpu.make_async_copy(src.at[:, from_at], whole.at[z, x_hi, core, :, to_at], sem[t]).start()

        def stage_swap():
            if by_x:
                return
            for t, (from_at, to_at) in enumerate(source(1 - x_lo)):
                unfinished.append(send(
                    src.at[:, from_at], whole.at[z, x_hi, core, :, to_at], sem[3 + t], sem[6 + t], x_mate
                ))

        def forward(step):
            zz = lax.rem(z + 8 - step, 8)
            if step < 4:
                unfinished.append(send(block(zz), block(zz), sem[9 + step], sem[13 + step], z_next))

        def backward(step):
            zz = lax.rem(z + step, 8)
            if step < 3:
                unfinished.append(send(block(zz), block(zz), sem[17 + step], sem[20 + step], z_prev))

        def to_core(ref):
            send(ref, ref, sem[23], sem[24], sibling)

        def first():
            for t, (from_at, to_at) in enumerate(source(x_lo)):
                part = whole.at[z, x_hi, core, :, to_at]
                pltpu.make_async_copy(part, part, sem[t]).wait()
                if not by_x:
                    arrived(whole.at[z, 1 - x_hi, core, :, to_at], sem[3 + t], sem[6 + t], x_mate)
            if name in FINE:
                for by in (4, 3, 5, 2, 6, 1, 7):
                    unfinished.append(send(block(z), block(z), sem[8 + by], sem[15 + by], (lat, at_lon(4 * by))))
                return
            forward(0)
            backward(0)
            if by_z:
                to_core(block(z))

        def along():
            mine = piece(0, slice(None))
            unfinished.append(send(mine, mine, sem[25], sem[26], after))
            unfinished.append(send(mine, mine, sem[27], sem[28], before))
            to_core(mine)

        def collect():
            for by in (1, 7, 2, 6, 3, 5, 4):
                arrived(block(lax.rem(z + 8 - by, 8)), sem[8 + by], sem[15 + by], z_next)
            along()

        def ring(step):
            zz = lax.rem(z + 8 - step, 8)
            arrived(block(zz), sem[9 + step - 1], sem[13 + step - 1], z_next)
            forward(step)
            if by_z:
                to_core(block(zz))
            if step < 4:
                zz = lax.rem(z + step, 8)
                arrived(block(zz), sem[17 + step - 1], sem[20 + step - 1], z_prev)
                backward(step)
                if by_z:
                    to_core(block(zz))
            elif not by_z:
                along()

        low, high = pl.ds(0, 4), pl.ds(4, 4)

        def second():
            theirs = piece(-1, slice(None))
            arrived(theirs, sem[25], sem[26], after)
            unfinished.append(send(piece(-1, low), piece(-1, low), sem[29], sem[30], after))
            to_core(theirs)
            theirs = piece(1, slice(None))
            arrived(theirs, sem[27], sem[28], before)
            unfinished.append(send(piece(1, high), piece(1, high), sem[31], sem[32], before))
            to_core(theirs)

        def third():
            arrived(piece(2, low), sem[29], sem[30], after)
            arrived(piece(2, high), sem[31], sem[32], before)
            to_core(piece(2, slice(None)))

        def ready():
            arrived(whole.at[:, :, 1 - core], sem[23], sem[24], sibling)

        def sent():
            pltpu.make_async_remote_copy(
                src_ref=whole.at[:, :, core], dst_ref=whole.at[:, :, core], send_sem=sem[23], recv_sem=sem[24],
                device_id=sibling, device_id_type=MESH,
            ).wait_send()

        steps = [first] + ([collect] if name in FINE else [functools.partial(ring, s) for s in range(1, 5)])
        if not by_z:
            steps += [second, third]
        return {"local": stage_local, "swap": stage_swap, "steps": steps, "ready": ready, "sent": sent}

    events = [weight_events(i) for i in range(len(WEIGHTS))]
    place = {spec[0]: i for i, spec in enumerate(WEIGHTS)}
    done = [0] * len(WEIGHTS)

    def advance(*names):
        for name in names:
            index = place[name]
            if done[index] < len(events[index]["steps"]):
                events[index]["steps"][done[index]]()
                done[index] += 1

    def finish(*names):
        for name in names:
            while done[place[name]] < len(events[place[name]]["steps"]):
                advance(name)
        for name in names:
            events[place[name]]["ready"]()

    def halo_send(number, table, rows_from, buffer, staging, devices):
        staging[...] = dot(table[...], rows_from).astype(BF16)
        for i, (at, count) in enumerate(PIECES):
            unfinished.append(send(
                staging.at[pl.ds(at, count)], buffer.at[pl.ds(NTOK + at, count)],
                halo_sems.at[number, i], halo_sems.at[number, 3 + i], devices[i],
            ))

    def halo_wait(number, buffer, devices):
        for i, (at, count) in enumerate(PIECES):
            arrived(buffer.at[pl.ds(NTOK + at, count)], halo_sems.at[number, i], halo_sems.at[number, 3 + i], devices[i])

    def pair_send(number, values, staging, buffer):
        staging[...] = jnp.concatenate([values, jnp.zeros((PAD - NMINE, values.shape[1]), F32)], axis=0).astype(BF16)
        unfinished.append(send(staging, buffer, pair_sems.at[number, 0], pair_sems.at[number, 1], pair_mate))

    def pair_wait(number, buffer):
        arrived(buffer, pair_sems.at[number, 0], pair_sems.at[number, 1], pair_mate)
        return buffer[...].astype(F32)[:NMINE]

    for event in events:
        event["local"]()
    barrier = pltpu.get_barrier_semaphore()
    for friend in friends:
        pl.semaphore_signal(barrier, inc=1, device_id=friend, device_id_type=MESH)
    xm = dot(to_merged[...], x_ref[...]).astype(BF16)
    xm_ref[...] = xm
    for buffer in (buf0, buf1, buf2, buf3):
        buffer[pl.ds(NTOK + HALO, NCAT - NTOK - HALO), :] = jnp.zeros((NCAT - NTOK - HALO, 512), BF16)
    buf0[pl.ds(0, NTOK), :] = xm
    pl.semaphore_wait(barrier, len(friends))
    for event in events[:4]:
        event["swap"]()
    halo_send(0, send_table, xm, buf0, sbuf0, behind)
    for event in events[4:]:
        event["swap"]()
    advance(*FINE)
    gm = dot(to_merged[...], g_ref[...]).astype(BF16)
    allowed = [dot(marks_ref[w], marks_ref[w], TRANS_B) for w in range(2)]
    advance(*FINE)
    advance("mwa", "mwb")
    halo_wait(0, buf0, behind)
    region = dot(region_table[...], buf0[...])
    unit, _ = normalise(region)
    region = (unit * gain_fine[...]).astype(BF16)
    advance(*FINE)
    advance("mwa", "mwb")
    advance(*FINE)
    advance("mwa", "mwb", "cq")
    finish("fq", "fk", "fv")

    def all_rows(ref, columns=slice(None)):
        value = ref[:, :, :, :, columns]
        return value.reshape(-1, value.shape[-1])

    for t, weight in enumerate((fq, fk, fv)):
        act[:, pl.ds(t * 512, 512)] = dot(region, all_rows(weight)).astype(BF16)
    advance("mwa", "mwb")
    heads = (0, 128, 512)
    then = (("mwa", "mwb", "co"), ("cq",), ("co",), ("cq", "spa", "spb"))
    for w in range(2):
        rows = pl.ds(w * NWIN, NWIN)
        for half in range(2):
            attend_forward(act, mixed, chances, rows, 8 * w, temper_fine, 0, allowed[w], heads, 2 * half, 2 * half + 2)
            advance(*then[2 * w + half])
    finish("fo")
    delta = dot(mixed[...], all_rows(fo)).astype(BF16)
    buf1[pl.ds(0, NTOK), :] = delta
    halo_send(1, halo_table, delta, buf1, sbuf1, ahead)
    advance("mwa", "mwb", "co", "spa", "spb", "cq")
    halo_wait(1, buf1, ahead)
    hidden = (xm_ref[...].astype(F32) + dot(back_table[...], buf1[...])).astype(BF16)
    hid[...] = hidden
    advance("mwa", "mwb", "co", "spa", "spb")

    def cells(values):
        return jnp.concatenate([values[NMINE * i:NMINE * (i + 1)] for i in range(4)], axis=1)

    unit, merge_scale = normalise(cells(hidden.astype(F32)))
    wide_ref[...] = unit
    mn_ref[...] = (unit * gain_merge[...]).astype(BF16)
    finish("mwa", "mwb")

    for n, weight in enumerate((mwa, mwb)):
        for half in range(2):
            part = pl.ds(half * 256, 256)
            coarse_ref[:, pl.ds(n * 512 + half * 256, 256)] = dot(mn_ref[...], all_rows(weight, part)).astype(BF16).astype(F32)
    advance("cq", "co", "spa", "spb")
    coarse = coarse_ref[...]
    coarse_unit, coarse_scale = normalise(coarse)
    coarse_norm = (coarse_unit * gain_coarse[...]).astype(BF16).astype(F32)
    pair_send(0, coarse_norm, psx, prx)
    advance("spa", "spb", "co")
    grad_cells = cells(gm.astype(F32)).astype(BF16)
    finish("cq")
    mine = [dot(coarse_norm.astype(BF16), all_rows(cq, pl.ds(t * 512, 512))) for t in range(3)]
    theirs = pair_wait(0, prx).astype(BF16)
    for t in range(3):
        part = pl.ds(t * 512, 512)
        cact[:, part] = jnp.concatenate([mine[t], dot(theirs, all_rows(cq, part))], axis=0).astype(BF16)
    for half in range(2):
        attend_forward(
            cact, cmixed, cchances, pl.ds(0, NWIN), 0, temper_coarse, 8 * x_lo, None, heads, 2 * half, 2 * half + 2
        )
        advance("co", "spa", "spb")
    finish("co")
    co_mine = co[pl.ds(4 * x_lo, 4)].reshape(512, 1024)
    mix = cmixed[...].astype(F32)
    pair_send(1, dot(mix[NMINE:].astype(BF16), co_mine), psy, pry)
    partial = dot(mix[:NMINE].astype(BF16), co_mine)
    finish("spa", "spb")

    def grad_step(n, carry):
        total = dot(grad_cells[:, :1024], spa[pl.ds(2 * n, 2)].reshape(256, 1024), TRANS_B)
        total += dot(grad_cells[:, 1024:], spb[pl.ds(2 * n, 2)].reshape(256, 1024), TRANS_B)
        gnext_ref[:, pl.ds(pl.multiple_of(n * 256, 256), 256)] = total.astype(BF16).astype(F32)
        return carry

    lax.fori_loop(0, 4, grad_step, 0)
    grad_next = gnext_ref[...]
    pair_send(2, grad_next, psz, prz)
    coarse_next = (coarse + (partial + pair_wait(1, pry))).astype(BF16)
    cnext_ref[...] = coarse_next

    for q in range(4):
        part = pl.ds(q % 2 * 512, 512)
        rows = pl.ds(q * NMINE, NMINE)
        wide_part = dot(cnext_ref[...], all_rows((spa, spb)[q // 2], part))
        gh_ref[rows, :] = hid[rows, :].astype(F32) + wide_part
    out_ref[...] = dot(from_merged[...], gh_ref[...].astype(BF16)).astype(BF16)

    grad_window = jnp.concatenate([grad_next, pair_wait(2, prz)], axis=0).astype(BF16)
    mixed[pl.ds(0, NWIN), :] = dot(grad_window, co_mine, TRANS_B).astype(BF16)
    attend_backward(cact, mixed, gact, cchances, pl.ds(0, NWIN), 0, temper_coarse, 8 * x_lo, heads)
    grad_act = gact[pl.ds(0, NWIN), :].astype(F32)

    def through_cq(rows):
        return jnp.concatenate([dot(rows, cq[pl.ds(2 * n, 2)].reshape(256, 1536), TRANS_B) for n in range(4)], axis=1)

    pair_send(3, through_cq(grad_act[NMINE:].astype(BF16)), psw, prw)
    partial = through_cq(grad_act[:NMINE].astype(BF16))
    grad_norm = (partial + pair_wait(3, prw)).astype(BF16).astype(F32)
    grad_coarse = (grad_next + norm_back(grad_norm, gain_coarse[...], coarse_unit, coarse_scale)).astype(BF16)
    grad_merged = jnp.concatenate(
        [
            dot(grad_coarse[:, :512], mwa[n].reshape(256, 512), TRANS_B)
            + dot(grad_coarse[:, 512:], mwb[n].reshape(256, 512), TRANS_B)
            for n in range(8)
        ],
        axis=1,
    ).astype(BF16).astype(F32)
    grad_merged = norm_back(grad_merged, gain_merge[...], wide_ref[...], merge_scale).astype(BF16).astype(F32)
    for q in range(4):
        rows = pl.ds(q * NMINE, NMINE)
        gh_ref[rows, :] = grad_merged[:, q * 512:(q + 1) * 512]
    grad_hidden = (gm.astype(F32) + gh_ref[...]).astype(BF16)
    hid[...] = grad_hidden

    buf2[pl.ds(0, NTOK), :] = grad_hidden
    halo_send(2, send_table, grad_hidden, buf2, sbuf2, behind)
    halo_wait(2, buf2, behind)
    grad_region = dot(region_table[...], buf2[...]).astype(BF16)
    mixed[...] = dot(grad_region, all_rows(fo), TRANS_B).astype(BF16)
    for w in range(2):
        attend_backward(act, mixed, gact, chances, pl.ds(w * NWIN, NWIN), 8 * w, temper_fine, 0, heads)
    grad_region = sum(
        dot(gact[:, pl.ds(t * 512, 512)], all_rows(weight), TRANS_B) for t, weight in enumerate((fq, fk, fv))
    ).astype(BF16)
    buf3[pl.ds(0, NTOK), :] = grad_region
    halo_send(3, halo_table, grad_region, buf3, sbuf3, ahead)
    unit, scale = normalise(xm_ref[...].astype(F32))
    halo_wait(3, buf3, ahead)
    grad_norm = dot(back_table[...], buf3[...]).astype(BF16).astype(F32)
    grad_in = hid[...].astype(F32) + norm_back(grad_norm, gain_fine[...], unit, scale)
    gin_ref[...] = dot(from_merged[...], grad_in.astype(BF16)).astype(BF16)

    for copy in unfinished:
        copy.wait_send()
    for event in events:
        event["sent"]()


def per_device(
    fine_tokens, grad_out, window_class, temper_fine, temper_coarse, gain_fine, fine_qkv, fine_out, gain_merge,
    merge_weight, gain_coarse, coarse_qkv, coarse_out, split_weight,
):
    at_pole = (lax.axis_index("lat") == lax.axis_size("lat") - 1) & (jnp.arange(ROWS) >= 3)
    labels = window_class + 3 * at_pole.astype(jnp.int32)[None, :, None]
    labels = labels.reshape(LEV, ROWS, 2, 12).transpose(2, 0, 1, 3).reshape(2, NWIN)
    marks = (labels[:, :, None] == jnp.arange(128)[None, None, :]).astype(BF16)
    vmem = pl.BlockSpec(memory_space=pltpu.VMEM)
    smem = pl.BlockSpec(memory_space=pltpu.SMEM)
    anyplace = pl.BlockSpec(memory_space=pl.ANY)
    scratch = [pltpu.VMEM((8, 2, 2, rows, cols), BF16) for _, rows, cols, _, _ in WEIGHTS]
    scratch += [pltpu.VMEM((NCAT, 512), BF16)] * 4 + [pltpu.VMEM((HALO, 512), BF16)] * 4
    scratch += [pltpu.VMEM((PAD, 1024), BF16)] * 8
    scratch += [
        pltpu.VMEM((NTOK, 512), BF16),
        pltpu.VMEM((NTOK, 1536), BF16),
        pltpu.VMEM((NTOK, 512), BF16),
        pltpu.VMEM((NTOK, 1536), BF16),
        pltpu.VMEM((16, NWIN, NWIN), F32),
        pltpu.VMEM((NTOK, 512), BF16),
        pltpu.VMEM((NWIN, 1536), BF16),
        pltpu.VMEM((NWIN, 512), BF16),
        pltpu.VMEM((8, NWIN, NWIN), F32),
        pltpu.VMEM((NMINE, 1024), F32),
        pltpu.VMEM((NMINE, 1024), BF16),
        pltpu.VMEM((NMINE, 1024), F32),
        pltpu.VMEM((NMINE, 2048), BF16),
        pltpu.VMEM((NMINE, 2048), F32),
        pltpu.VMEM((NTOK, 512), F32),
        pltpu.SemaphoreType.DMA((len(WEIGHTS), SEMS_PER_WEIGHT)),
        pltpu.SemaphoreType.DMA((4, 6)),
        pltpu.SemaphoreType.DMA((4, 2)),
    ]
    tables = layout_tables()
    output, grad_in = pl.pallas_call(
        kernel,
        out_shape=[jax.ShapeDtypeStruct((NTOK, 512), BF16)] * 2,
        in_specs=[vmem] * 3 + [smem] * 2 + [vmem] * 3 + [anyplace] * 6 + [vmem] * 6,
        out_specs=[vmem] * 2,
        scratch_shapes=scratch,
        compiler_params=pltpu.CompilerParams(
            collective_id=0, has_side_effects=True, vmem_limit_bytes=56 * 1024 * 1024
        ),
    )(
        fine_tokens.reshape(NTOK, 512), grad_out.reshape(NTOK, 512), marks, temper_fine, temper_coarse,
        gain_fine.reshape(1, -1), gain_merge.reshape(1, -1), gain_coarse.reshape(1, -1),
        fine_qkv, fine_out, merge_weight, coarse_qkv, coarse_out, split_weight, *tables,
    )
    return output.reshape(fine_tokens.shape), grad_in.reshape(fine_tokens.shape)


def solution(mesh):
    tiles = P(None, "lat", "lon", None)
    shards = P("lon", None)
    return jax.shard_map(
        per_device,
        mesh=mesh,
        in_specs=(
            tiles, tiles, P(None, "lat", "lon"), P(), P(), P(), shards, shards, P(), shards, P(), shards, shards, shards,
        ),
        out_specs=(tiles, tiles),
        check_vma=False,
    )
```

```python
import functools

import jax
import jax.numpy as jnp
import numpy as np
from jax import lax
from jax.experimental import pallas as pl
from jax.experimental.pallas import tpu as pltpu
from jax.sharding import PartitionSpec as P

MESH = pl.DeviceIdType.MESH
F32, BF16 = jnp.float32, jnp.bfloat16
LN_EPS = 1e-05
UNIT_EPS = 1e-06

LEV, ROWS, COLS = 2, 6, 24
NTOK = LEV * ROWS * COLS
NWIN = 144
NMINE = 72
HALO = 208
NCAT = 512
PIECES = ((0, 112), (112, 48), (160, 48))
PAD = 80


def layout_tables():
    flat = np.arange(NTOK).reshape(LEV, ROWS, COLS)
    merged_of = np.zeros(NTOK, np.int64)
    order = np.concatenate([flat[:, di::2, dj::2].reshape(-1) for dj in (0, 1) for di in (0, 1)])
    merged_of[order] = np.arange(NTOK)
    to_merged = np.zeros((NTOK, NTOK), np.float32)
    to_merged[np.arange(NTOK), order] = 1
    halo_slot = {}
    at = {"lat": 0, "lon": 112, "diag": 160}
    send = np.zeros((HALO, NTOK), np.float32)
    for l in range(LEV):
        for i in range(ROWS):
            for j in range(COLS):
                kind = {(1, 0): "lat", (0, 1): "lon", (1, 1): "diag"}.get((int(i < 3), int(j < 6)))
                if kind:
                    halo_slot[l, i, j] = at[kind]
                    send[at[kind], merged_of[flat[l, i, j]]] = 1
                    at[kind] += 1
    region = np.zeros((NTOK, NCAT), np.float32)
    row = 0
    for w in range(2):
        for l in range(LEV):
            for i in range(ROWS):
                for j in range(12):
                    si, sj = i + 3, 12 * w + j + 6
                    if si < ROWS and sj < COLS:
                        region[row, merged_of[flat[l, si, sj]]] = 1
                    else:
                        region[row, NTOK + halo_slot[l, si % ROWS, sj % COLS]] = 1
                    row += 1
    own, halo = region[:, :NTOK], region[:, NTOK:NTOK + HALO]
    back = np.zeros((NTOK, NCAT), np.float32)
    back[:, :NTOK] = own.T
    back[:, NTOK:NTOK + HALO] = send.T
    tables = (to_merged, to_merged.T, send, region, back, halo.T)
    return [np.ascontiguousarray(t).astype(jnp.bfloat16) for t in tables]


def dot(a, b, dims=((1,), (0,))):
    return lax.dot_general(a, b, (dims, ((), ())), preferred_element_type=F32)


TRANS_B = ((1,), (1,))
TRANS_A = ((0,), (0,))


def normalise(values):
    average = jnp.mean(values, axis=-1, keepdims=True)
    centred = values - average
    scale = lax.rsqrt(jnp.mean(centred * centred, axis=-1, keepdims=True) + LN_EPS)
    return centred * scale, scale


def norm_back(grad, gains, unit, scale):
    grad = grad * gains
    part = jnp.mean(grad, axis=-1, keepdims=True)
    along = jnp.mean(grad * unit, axis=-1, keepdims=True)
    return scale * (grad - part - unit * along)


def half_mask(rows):
    return lax.broadcasted_iota(jnp.int32, (rows, 128), 1) < 64


def half_sums(values, low):
    first = jnp.sum(jnp.where(low, values, 0.0), axis=-1, keepdims=True)
    second = jnp.sum(jnp.where(low, 0.0, values), axis=-1, keepdims=True)
    return jnp.where(low, first, second)


def head_columns(p, heads):
    first, step, kind = heads
    return [pl.ds(pl.multiple_of(first + p * step + t * kind, 128), 128) for t in range(3)]


def attend_forward(act, mixed, chances, rows, first, temper, temper_at, allowed, heads, start, stop):
    low = half_mask(NWIN)

    def pair(p, carry):
        q, k, v = (act[rows, s] for s in head_columns(p, heads))
        q, k = q.astype(F32), k.astype(F32)
        q = q * lax.rsqrt(half_sums(q * q, low) + UNIT_EPS)
        k = (k * lax.rsqrt(half_sums(k * k, low) + UNIT_EPS)).astype(BF16)
        mixes = []
        for j in range(2):
            mine = low if j == 0 else jnp.logical_not(low)
            scores = dot(jnp.where(mine, q, 0.0).astype(BF16), k, TRANS_B) * temper[temper_at + 2 * p + j]
            weights = jnp.exp(scores)
            if allowed is not None:
                weights = weights * allowed
            chance = weights * (1.0 / jnp.sum(weights, axis=-1, keepdims=True))
            chances[first + 2 * p + j] = chance
            mixes.append(dot(chance.astype(BF16), v))
        mixed[rows, pl.ds(pl.multiple_of(p * 128, 128), 128)] = jnp.where(low, mixes[0], mixes[1]).astype(BF16)
        return carry

    lax.fori_loop(start, stop, pair, 0, unroll=2)


def attend_backward(act, grad_mixed, grad_act, chances, rows, first, temper, temper_at, heads):
    low = half_mask(NWIN)

    def pair(p, carry):
        at = head_columns(p, heads)
        q, k, v = (act[rows, s].astype(F32) for s in at)
        q_scale = lax.rsqrt(half_sums(q * q, low) + UNIT_EPS)
        k_scale = lax.rsqrt(half_sums(k * k, low) + UNIT_EPS)
        q, k = q * q_scale, k * k_scale
        q_low, k_low = q.astype(BF16), k.astype(BF16)
        grad = grad_mixed[rows, pl.ds(pl.multiple_of(p * 128, 128), 128)]
        gq, gk, gv = [], [], []
        for j in range(2):
            mine = low if j == 0 else jnp.logical_not(low)
            chance = chances[first + 2 * p + j]
            gc = dot(grad, jnp.where(mine, v, 0.0).astype(BF16), TRANS_B)
            gc = chance * (gc - jnp.sum(gc * chance, axis=-1, keepdims=True))
            gs = (gc * temper[temper_at + 2 * p + j]).astype(BF16)
            gq.append(dot(gs, k_low))
            gk.append(dot(gs, q_low, TRANS_A))
            gv.append(dot(chance.astype(BF16), grad, TRANS_A))
        gq, gk, gv = (jnp.where(low, *parts) for parts in (gq, gk, gv))
        grad_act[rows, at[0]] = (q_scale * (gq - q * half_sums(gq * q, low))).astype(BF16)
        grad_act[rows, at[1]] = (k_scale * (gk - k * half_sums(gk * k, low))).astype(BF16)
        grad_act[rows, at[2]] = gv.astype(BF16)
        return carry

    lax.fori_loop(0, 4, pair, 0, unroll=2)


WEIGHTS = (
    ("fk", 16, 512, "x", 512),
    ("fo", 16, 512, "x", 0),
    ("fq", 16, 512, "y", 0),
    ("fv", 16, 512, "y", 1024),
    ("mwa", 64, 512, "x", 0),
    ("mwb", 64, 512, "y", 512),
    ("cq", 32, 1536, "z", None),
    ("co", 32, 1024, "x", 0),
    ("spa", 32, 1024, "x", 0),
    ("spb", 32, 1024, "y", 1024),
)
FINE = ("fk", "fo", "fq", "fv")
SEMS_PER_WEIGHT = 33


def kernel(
    x_ref, g_ref, marks_ref, temper_fine, temper_coarse, gain_fine, gain_merge, gain_coarse,
    fq_in, fo_in, mw_in, cq_in, co_in, sp_in,
    to_merged, from_merged, send_table, region_table, back_table, halo_table,
    out_ref, gin_ref,
    fk, fo, fq, fv, mwa, mwb, cq, co, spa, spb,
    buf0, buf1, buf2, buf3, sbuf0, sbuf1, sbuf2, sbuf3,
    prx, pry, prz, prw, psx, psy, psz, psw,
    xm_ref, act, mixed, gact, chances, hid, cact, cmixed, cchances, coarse_ref, cnext_ref, gnext_ref, mn_ref, wide_ref, gh_ref,
    sems, halo_sems, pair_sems,
):
    lat, lon = lax.axis_index("lat"), lax.axis_index("lon")
    y, x_lo = lat // 2, lat % 2
    z, x_hi, core = lon // 4, (lon // 2) % 2, lon % 2

    def at_lat(by):
        return lax.rem(lat + 8 + by, 8)

    def at_lon(by):
        return lax.rem(lon + 32 + by, 32)

    z_next, z_prev = (lat, at_lon(4)), (lat, at_lon(-4))
    y_next, y_prev = (at_lat(2), lon), (at_lat(-2), lon)
    x = 2 * x_hi + x_lo

    def at_x(by):
        there = lax.rem(x + 4 + by, 4)
        return (2 * y + lax.rem(there, 2), 4 * z + 2 * (there // 2) + core)

    x_next, x_prev = at_x(1), at_x(-1)
    x_mate = (lat + 1 - 2 * x_lo, lon + 2 - 4 * x_hi)
    sibling = (lat, lon + 1 - 2 * core)
    pair_mate = (lat + 1 - 2 * x_lo, lon)
    behind = ((at_lat(-1), lon), (lat, at_lon(-1)), (at_lat(-1), at_lon(-1)))
    ahead = ((at_lat(1), lon), (lat, at_lon(1)), (at_lat(1), at_lon(1)))
    z_all = tuple((lat, at_lon(4 * by)) for by in range(1, 8))
    friends = z_all + (y_next, y_prev, x_next, x_prev, x_mate) + behind + ahead

    unfinished = []

    def send(src, dst, sem_out, sem_in, device):
        copy = pltpu.make_async_remote_copy(
            src_ref=src, dst_ref=dst, send_sem=sem_out, recv_sem=sem_in, device_id=device, device_id_type=MESH
        )
        copy.start()
        return copy

    def arrived(dst, sem_out, sem_in, device):
        pltpu.make_async_remote_copy(
            src_ref=dst, dst_ref=dst, send_sem=sem_out, recv_sem=sem_in, device_id=device, device_id_type=MESH
        ).wait_recv()

    inputs = (fq_in, fo_in, fq_in, fq_in, mw_in, mw_in, cq_in, co_in, sp_in, sp_in)
    buffers = (fk, fo, fq, fv, mwa, mwb, cq, co, spa, spb)

    def weight_events(index):
        name, rows, cols, axis, base = WEIGHTS[index]
        src, whole = inputs[index], buffers[index]
        by_x, by_z = axis == "x", axis == "z"
        width = {"x": cols // 2, "y": cols // 4, "z": cols}[axis]
        at, after, before = (x, x_next, x_prev) if by_x else (y, y_next, y_prev)
        sem = [sems.at[index, i] for i in range(SEMS_PER_WEIGHT)]

        def lanes(part):
            return pl.ds(pl.multiple_of(part * width, 128), width)

        def piece(by, levels):
            there = lax.rem(at + 4 + by, 4)
            if by_z:
                return whole.at[levels, :, core]
            if by_x:
                return whole.at[levels, there // 2, core, :, lanes(lax.rem(there, 2))]
            return whole.at[levels, :, core, :, lanes(there)]

        def block(zz):
            return piece(0, zz)

        def source(parity):
            if by_z:
                return [
                    (pl.ds(pl.multiple_of(t * 1024 + parity * 512, 128), 512), pl.ds(t * 512, 512)) for t in range(3)
                ]
            part = x_lo if by_x else y
            return [(pl.ds(pl.multiple_of(base + part * width, 128), width), lanes(part))]

        def stage_local():
            for t, (from_at, to_at) in enumerate(source(x_lo)):
                pltpu.make_async_copy(src.at[:, from_at], whole.at[z, x_hi, core, :, to_at], sem[t]).start()

        def stage_swap():
            if by_x:
                return
            for t, (from_at, to_at) in enumerate(source(1 - x_lo)):
                unfinished.append(send(
                    src.at[:, from_at], whole.at[z, x_hi, core, :, to_at], sem[3 + t], sem[6 + t], x_mate
                ))

        def forward(step):
            zz = lax.rem(z + 8 - step, 8)
            if step < 4:
                unfinished.append(send(block(zz), block(zz), sem[9 + step], sem[13 + step], z_next))

        def backward(step):
            zz = lax.rem(z + step, 8)
            if step < 3:
                unfinished.append(send(block(zz), block(zz), sem[17 + step], sem[20 + step], z_prev))

        def to_core(ref):
            send(ref, ref, sem[23], sem[24], sibling)

        def first():
            for t, (from_at, to_at) in enumerate(source(x_lo)):
                part = whole.at[z, x_hi, core, :, to_at]
                pltpu.make_async_copy(part, part, sem[t]).wait()
                if not by_x:
                    arrived(whole.at[z, 1 - x_hi, core, :, to_at], sem[3 + t], sem[6 + t], x_mate)
            if name in FINE:
                for by in (4, 3, 5, 2, 6, 1, 7):
                    unfinished.append(send(block(z), block(z), sem[8 + by], sem[15 + by], (lat, at_lon(4 * by))))
                return
            forward(0)
            backward(0)
            if by_z:
                to_core(block(z))

        def along():
            mine = piece(0, slice(None))
            unfinished.append(send(mine, mine, sem[25], sem[26], after))
            unfinished.append(send(mine, mine, sem[27], sem[28], before))
            to_core(mine)

        def collect():
            for by in (1, 7, 2, 6, 3, 5, 4):
                arrived(block(lax.rem(z + 8 - by, 8)), sem[8 + by], sem[15 + by], z_next)
            along()

        def ring(step):
            zz = lax.rem(z + 8 - step, 8)
            arrived(block(zz), sem[9 + step - 1], sem[13 + step - 1], z_next)
            forward(step)
            if by_z:
                to_core(block(zz))
            if step < 4:
                zz = lax.rem(z + step, 8)
                arrived(block(zz), sem[17 + step - 1], sem[20 + step - 1], z_prev)
                backward(step)
                if by_z:
                    to_core(block(zz))
            elif not by_z:
                along()

        low, high = pl.ds(0, 4), pl.ds(4, 4)

        def second():
            theirs = piece(-1, slice(None))
            arrived(theirs, sem[25], sem[26], after)
            unfinished.append(send(piece(-1, low), piece(-1, low), sem[29], sem[30], after))
            to_core(theirs)
            theirs = piece(1, slice(None))
            arrived(theirs, sem[27], sem[28], before)
            unfinished.append(send(piece(1, high), piece(1, high), sem[31], sem[32], before))
            to_core(theirs)

        def third():
            arrived(piece(2, low), sem[29], sem[30], after)
            arrived(piece(2, high), sem[31], sem[32], before)
            to_core(piece(2, slice(None)))

        def ready():
            arrived(whole.at[:, :, 1 - core], sem[23], sem[24], sibling)

        def sent():
            pltpu.make_async_remote_copy(
                src_ref=whole.at[:, :, core], dst_ref=whole.at[:, :, core], send_sem=sem[23], recv_sem=sem[24],
                device_id=sibling, device_id_type=MESH,
            ).wait_send()

        steps = [first] + ([collect] if name in FINE else [functools.partial(ring, s) for s in range(1, 5)])
        if not by_z:
            steps += [second, third]
        return {"local": stage_local, "swap": stage_swap, "steps": steps, "ready": ready, "sent": sent}

    events = [weight_events(i) for i in range(len(WEIGHTS))]
    place = {spec[0]: i for i, spec in enumerate(WEIGHTS)}
    done = [0] * len(WEIGHTS)

    def advance(*names):
        for name in names:
            index = place[name]
            if done[index] < len(events[index]["steps"]):
                events[index]["steps"][done[index]]()
                done[index] += 1

    def finish(*names):
        for name in names:
            while done[place[name]] < len(events[place[name]]["steps"]):
                advance(name)
        for name in names:
            events[place[name]]["ready"]()

    def halo_send(number, table, rows_from, buffer, staging, devices):
        staging[...] = dot(table[...], rows_from).astype(BF16)
        for i, (at, count) in enumerate(PIECES):
            unfinished.append(send(
                staging.at[pl.ds(at, count)], buffer.at[pl.ds(NTOK + at, count)],
                halo_sems.at[number, i], halo_sems.at[number, 3 + i], devices[i],
            ))

    def halo_wait(number, buffer, devices):
        for i, (at, count) in enumerate(PIECES):
            arrived(buffer.at[pl.ds(NTOK + at, count)], halo_sems.at[number, i], halo_sems.at[number, 3 + i], devices[i])

    def pair_send(number, values, staging, buffer):
        staging[...] = jnp.concatenate([values, jnp.zeros((PAD - NMINE, values.shape[1]), F32)], axis=0).astype(BF16)
        unfinished.append(send(staging, buffer, pair_sems.at[number, 0], pair_sems.at[number, 1], pair_mate))

    def pair_wait(number, buffer):
        arrived(buffer, pair_sems.at[number, 0], pair_sems.at[number, 1], pair_mate)
        return buffer[...].astype(F32)[:NMINE]

    for event in events:
        event["local"]()
    barrier = pltpu.get_barrier_semaphore()
    for friend in friends:
        pl.semaphore_signal(barrier, inc=1, device_id=friend, device_id_type=MESH)
    xm = dot(to_merged[...], x_ref[...]).astype(BF16)
    xm_ref[...] = xm
    for buffer in (buf0, buf1, buf2, buf3):
        buffer[pl.ds(NTOK + HALO, NCAT - NTOK - HALO), :] = jnp.zeros((NCAT - NTOK - HALO, 512), BF16)
    buf0[pl.ds(0, NTOK), :] = xm
    pl.semaphore_wait(barrier, len(friends))
    for event in events[:4]:
        event["swap"]()
    halo_send(0, send_table, xm, buf0, sbuf0, behind)
    for event in events[4:]:
        event["swap"]()
    advance(*FINE)
    gm = dot(to_merged[...], g_ref[...]).astype(BF16)
    allowed = [dot(marks_ref[w], marks_ref[w], TRANS_B) for w in range(2)]
    advance(*FINE)
    advance("mwa", "mwb", "co")
    halo_wait(0, buf0, behind)
    region = dot(region_table[...], buf0[...])
    unit, _ = normalise(region)
    region = (unit * gain_fine[...]).astype(BF16)
    advance(*FINE)
    advance("mwa", "mwb", "co")
    advance(*FINE)
    advance("mwa", "mwb", "co", "cq")
    finish("fq", "fk", "fv")

    def all_rows(ref, columns=slice(None)):
        value = ref[:, :, :, :, columns]
        return value.reshape(-1, value.shape[-1])

    for t, weight in enumerate((fq, fk, fv)):
        act[:, pl.ds(t * 512, 512)] = dot(region, all_rows(weight)).astype(BF16)
    advance("mwa", "mwb", "co")
    heads = (0, 128, 512)
    then = (("mwa", "mwb", "co", "spa", "spb"), ("cq", "spa", "spb"), ("spa", "spb"), ("cq", "spa", "spb"))
    for w in range(2):
        rows = pl.ds(w * NWIN, NWIN)
        for half in range(2):
            attend_forward(act, mixed, chances, rows, 8 * w, temper_fine, 0, allowed[w], heads, 2 * half, 2 * half + 2)
            advance(*then[2 * w + half])
    finish("fo")
    delta = dot(mixed[...], all_rows(fo)).astype(BF16)
    buf1[pl.ds(0, NTOK), :] = delta
    halo_send(1, halo_table, delta, buf1, sbuf1, ahead)
    advance("mwa", "mwb", "spa", "spb", "cq")
    halo_wait(1, buf1, ahead)
    hidden = (xm_ref[...].astype(F32) + dot(back_table[...], buf1[...])).astype(BF16)
    hid[...] = hidden
    advance("mwa", "mwb", "co")

    def cells(values):
        return jnp.concatenate([values[NMINE * i:NMINE * (i + 1)] for i in range(4)], axis=1)

    unit, merge_scale = normalise(cells(hidden.astype(F32)))
    wide_ref[...] = unit
    mn_ref[...] = (unit * gain_merge[...]).astype(BF16)
    finish("mwa", "mwb")

    for n, weight in enumerate((mwa, mwb)):
        for half in range(2):
            part = pl.ds(half * 256, 256)
            coarse_ref[:, pl.ds(n * 512 + half * 256, 256)] = dot(mn_ref[...], all_rows(weight, part)).astype(BF16).astype(F32)
    advance("cq", "co", "spa", "spb")
    coarse = coarse_ref[...]
    coarse_unit, coarse_scale = normalise(coarse)
    coarse_norm = (coarse_unit * gain_coarse[...]).astype(BF16).astype(F32)
    pair_send(0, coarse_norm, psx, prx)
    advance("spa", "spb", "co")
    grad_cells = cells(gm.astype(F32)).astype(BF16)
    finish("cq")
    mine = [dot(coarse_norm.astype(BF16), all_rows(cq, pl.ds(t * 512, 512))) for t in range(3)]
    theirs = pair_wait(0, prx).astype(BF16)
    for t in range(3):
        part = pl.ds(t * 512, 512)
        cact[:, part] = jnp.concatenate([mine[t], dot(theirs, all_rows(cq, part))], axis=0).astype(BF16)
    for half in range(2):
        attend_forward(
            cact, cmixed, cchances, pl.ds(0, NWIN), 0, temper_coarse, 8 * x_lo, None, heads, 2 * half, 2 * half + 2
        )
        advance("co", "spa", "spb")
    finish("co")
    co_mine = co[pl.ds(4 * x_lo, 4)].reshape(512, 1024)
    mix = cmixed[...].astype(F32)
    pair_send(1, dot(mix[NMINE:].astype(BF16), co_mine), psy, pry)
    partial = dot(mix[:NMINE].astype(BF16), co_mine)
    finish("spa", "spb")

    def grad_step(n, carry):
        total = dot(grad_cells[:, :1024], spa[pl.ds(2 * n, 2)].reshape(256, 1024), TRANS_B)
        total += dot(grad_cells[:, 1024:], spb[pl.ds(2 * n, 2)].reshape(256, 1024), TRANS_B)
        gnext_ref[:, pl.ds(pl.multiple_of(n * 256, 256), 256)] = total.astype(BF16).astype(F32)
        return carry

    lax.fori_loop(0, 4, grad_step, 0)
    grad_next = gnext_ref[...]
    pair_send(2, grad_next, psz, prz)
    coarse_next = (coarse + (partial + pair_wait(1, pry))).astype(BF16)
    cnext_ref[...] = coarse_next

    for q in range(4):
        part = pl.ds(q % 2 * 512, 512)
        rows = pl.ds(q * NMINE, NMINE)
        wide_part = dot(cnext_ref[...], all_rows((spa, spb)[q // 2], part))
        gh_ref[rows, :] = hid[rows, :].astype(F32) + wide_part
    out_ref[...] = dot(from_merged[...], gh_ref[...].astype(BF16)).astype(BF16)

    grad_window = jnp.concatenate([grad_next, pair_wait(2, prz)], axis=0).astype(BF16)
    mixed[pl.ds(0, NWIN), :] = dot(grad_window, co_mine, TRANS_B).astype(BF16)
    attend_backward(cact, mixed, gact, cchances, pl.ds(0, NWIN), 0, temper_coarse, 8 * x_lo, heads)
    grad_act = gact[pl.ds(0, NWIN), :].astype(F32)

    def through_cq(rows):
        return jnp.concatenate([dot(rows, cq[pl.ds(2 * n, 2)].reshape(256, 1536), TRANS_B) for n in range(4)], axis=1)

    pair_send(3, through_cq(grad_act[NMINE:].astype(BF16)), psw, prw)
    partial = through_cq(grad_act[:NMINE].astype(BF16))
    grad_norm = (partial + pair_wait(3, prw)).astype(BF16).astype(F32)
    grad_coarse = (grad_next + norm_back(grad_norm, gain_coarse[...], coarse_unit, coarse_scale)).astype(BF16)
    grad_merged = jnp.concatenate(
        [
            dot(grad_coarse[:, :512], mwa[n].reshape(256, 512), TRANS_B)
            + dot(grad_coarse[:, 512:], mwb[n].reshape(256, 512), TRANS_B)
            for n in range(8)
        ],
        axis=1,
    ).astype(BF16).astype(F32)
    grad_merged = norm_back(grad_merged, gain_merge[...], wide_ref[...], merge_scale).astype(BF16).astype(F32)
    for q in range(4):
        rows = pl.ds(q * NMINE, NMINE)
        gh_ref[rows, :] = grad_merged[:, q * 512:(q + 1) * 512]
    grad_hidden = (gm.astype(F32) + gh_ref[...]).astype(BF16)
    hid[...] = grad_hidden

    buf2[pl.ds(0, NTOK), :] = grad_hidden
    halo_send(2, send_table, grad_hidden, buf2, sbuf2, behind)
    halo_wait(2, buf2, behind)
    grad_region = dot(region_table[...], buf2[...]).astype(BF16)
    mixed[...] = dot(grad_region, all_rows(fo), TRANS_B).astype(BF16)
    for w in range(2):
        attend_backward(act, mixed, gact, chances, pl.ds(w * NWIN, NWIN), 8 * w, temper_fine, 0, heads)
    grad_region = sum(
        dot(gact[:, pl.ds(t * 512, 512)], all_rows(weight), TRANS_B) for t, weight in enumerate((fq, fk, fv))
    ).astype(BF16)
    buf3[pl.ds(0, NTOK), :] = grad_region
    halo_send(3, halo_table, grad_region, buf3, sbuf3, ahead)
    unit, scale = normalise(xm_ref[...].astype(F32))
    halo_wait(3, buf3, ahead)
    grad_norm = dot(back_table[...], buf3[...]).astype(BF16).astype(F32)
    grad_in = hid[...].astype(F32) + norm_back(grad_norm, gain_fine[...], unit, scale)
    gin_ref[...] = dot(from_merged[...], grad_in.astype(BF16)).astype(BF16)

    for copy in unfinished:
        copy.wait_send()
    for event in events:
        event["sent"]()


def per_device(
    fine_tokens, grad_out, window_class, temper_fine, temper_coarse, gain_fine, fine_qkv, fine_out, gain_merge,
    merge_weight, gain_coarse, coarse_qkv, coarse_out, split_weight,
):
    at_pole = (lax.axis_index("lat") == lax.axis_size("lat") - 1) & (jnp.arange(ROWS) >= 3)
    labels = window_class + 3 * at_pole.astype(jnp.int32)[None, :, None]
    labels = labels.reshape(LEV, ROWS, 2, 12).transpose(2, 0, 1, 3).reshape(2, NWIN)
    marks = (labels[:, :, None] == jnp.arange(128)[None, None, :]).astype(BF16)
    vmem = pl.BlockSpec(memory_space=pltpu.VMEM)
    smem = pl.BlockSpec(memory_space=pltpu.SMEM)
    anyplace = pl.BlockSpec(memory_space=pl.ANY)
    scratch = [pltpu.VMEM((8, 2, 2, rows, cols), BF16) for _, rows, cols, _, _ in WEIGHTS]
    scratch += [pltpu.VMEM((NCAT, 512), BF16)] * 4 + [pltpu.VMEM((HALO, 512), BF16)] * 4
    scratch += [pltpu.VMEM((PAD, 1024), BF16)] * 8
    scratch += [
        pltpu.VMEM((NTOK, 512), BF16),
        pltpu.VMEM((NTOK, 1536), BF16),
        pltpu.VMEM((NTOK, 512), BF16),
        pltpu.VMEM((NTOK, 1536), BF16),
        pltpu.VMEM((16, NWIN, NWIN), F32),
        pltpu.VMEM((NTOK, 512), BF16),
        pltpu.VMEM((NWIN, 1536), BF16),
        pltpu.VMEM((NWIN, 512), BF16),
        pltpu.VMEM((8, NWIN, NWIN), F32),
        pltpu.VMEM((NMINE, 1024), F32),
        pltpu.VMEM((NMINE, 1024), BF16),
        pltpu.VMEM((NMINE, 1024), F32),
        pltpu.VMEM((NMINE, 2048), BF16),
        pltpu.VMEM((NMINE, 2048), F32),
        pltpu.VMEM((NTOK, 512), F32),
        pltpu.SemaphoreType.DMA((len(WEIGHTS), SEMS_PER_WEIGHT)),
        pltpu.SemaphoreType.DMA((4, 6)),
        pltpu.SemaphoreType.DMA((4, 2)),
    ]
    tables = layout_tables()
    output, grad_in = pl.pallas_call(
        kernel,
        out_shape=[jax.ShapeDtypeStruct((NTOK, 512), BF16)] * 2,
        in_specs=[vmem] * 3 + [smem] * 2 + [vmem] * 3 + [anyplace] * 6 + [vmem] * 6,
        out_specs=[vmem] * 2,
        scratch_shapes=scratch,
        compiler_params=pltpu.CompilerParams(
            collective_id=0, has_side_effects=True, vmem_limit_bytes=56 * 1024 * 1024
        ),
    )(
        fine_tokens.reshape(NTOK, 512), grad_out.reshape(NTOK, 512), marks, temper_fine, temper_coarse,
        gain_fine.reshape(1, -1), gain_merge.reshape(1, -1), gain_coarse.reshape(1, -1),
        fine_qkv, fine_out, merge_weight, coarse_qkv, coarse_out, split_weight, *tables,
    )
    return output.reshape(fine_tokens.shape), grad_in.reshape(fine_tokens.shape)


def solution(mesh):
    tiles = P(None, "lat", "lon", None)
    shards = P("lon", None)
    return jax.shard_map(
        per_device,
        mesh=mesh,
        in_specs=(
            tiles, tiles, P(None, "lat", "lon"), P(), P(), P(), shards, shards, P(), shards, P(), shards, shards, shards,
        ),
        out_specs=(tiles, tiles),
        check_vma=False,
    )
```

```python
import functools

import jax
import jax.numpy as jnp
import numpy as np
from jax import lax
from jax.experimental import pallas as pl
from jax.experimental.pallas import tpu as pltpu
from jax.sharding import PartitionSpec as P

MESH = pl.DeviceIdType.MESH
F32, BF16 = jnp.float32, jnp.bfloat16
LN_EPS = 1e-05
UNIT_EPS = 1e-06

LEV, ROWS, COLS = 2, 6, 24
NTOK = LEV * ROWS * COLS
NWIN = 144
NMINE = 72
HALO = 208
NCAT = 512
PIECES = ((0, 112), (112, 48), (160, 48))
PAD = 80


def layout_tables():
    flat = np.arange(NTOK).reshape(LEV, ROWS, COLS)
    merged_of = np.zeros(NTOK, np.int64)
    order = np.concatenate([flat[:, di::2, dj::2].reshape(-1) for dj in (0, 1) for di in (0, 1)])
    merged_of[order] = np.arange(NTOK)
    to_merged = np.zeros((NTOK, NTOK), np.float32)
    to_merged[np.arange(NTOK), order] = 1
    halo_slot = {}
    at = {"lat": 0, "lon": 112, "diag": 160}
    send = np.zeros((HALO, NTOK), np.float32)
    for l in range(LEV):
        for i in range(ROWS):
            for j in range(COLS):
                kind = {(1, 0): "lat", (0, 1): "lon", (1, 1): "diag"}.get((int(i < 3), int(j < 6)))
                if kind:
                    halo_slot[l, i, j] = at[kind]
                    send[at[kind], merged_of[flat[l, i, j]]] = 1
                    at[kind] += 1
    region = np.zeros((NTOK, NCAT), np.float32)
    row = 0
    for w in range(2):
        for l in range(LEV):
            for i in range(ROWS):
                for j in range(12):
                    si, sj = i + 3, 12 * w + j + 6
                    if si < ROWS and sj < COLS:
                        region[row, merged_of[flat[l, si, sj]]] = 1
                    else:
                        region[row, NTOK + halo_slot[l, si % ROWS, sj % COLS]] = 1
                    row += 1
    own, halo = region[:, :NTOK], region[:, NTOK:NTOK + HALO]
    back = np.zeros((NTOK, NCAT), np.float32)
    back[:, :NTOK] = own.T
    back[:, NTOK:NTOK + HALO] = send.T
    tables = (to_merged, to_merged.T, send, region, back, halo.T)
    return [np.ascontiguousarray(t).astype(jnp.bfloat16) for t in tables]


def dot(a, b, dims=((1,), (0,))):
    return lax.dot_general(a, b, (dims, ((), ())), preferred_element_type=F32)


TRANS_B = ((1,), (1,))
TRANS_A = ((0,), (0,))


def normalise(values):
    average = jnp.mean(values, axis=-1, keepdims=True)
    centred = values - average
    scale = lax.rsqrt(jnp.mean(centred * centred, axis=-1, keepdims=True) + LN_EPS)
    return centred * scale, scale


def norm_back(grad, gains, unit, scale):
    grad = grad * gains
    part = jnp.mean(grad, axis=-1, keepdims=True)
    along = jnp.mean(grad * unit, axis=-1, keepdims=True)
    return scale * (grad - part - unit * along)


def half_mask(rows):
    return lax.broadcasted_iota(jnp.int32, (rows, 128), 1) < 64


def half_sums(values, low):
    first = jnp.sum(jnp.where(low, values, 0.0), axis=-1, keepdims=True)
    second = jnp.sum(jnp.where(low, 0.0, values), axis=-1, keepdims=True)
    return jnp.where(low, first, second)


def head_columns(p, heads):
    first, step, kind = heads
    return [pl.ds(pl.multiple_of(first + p * step + t * kind, 128), 128) for t in range(3)]


def attend_forward(act, mixed, chances, rows, first, temper, temper_at, allowed, heads, start, stop):
    low = half_mask(NWIN)

    def pair(p, carry):
        q, k, v = (act[rows, s] for s in head_columns(p, heads))
        q, k = q.astype(F32), k.astype(F32)
        q = q * lax.rsqrt(half_sums(q * q, low) + UNIT_EPS)
        k = (k * lax.rsqrt(half_sums(k * k, low) + UNIT_EPS)).astype(BF16)
        mixes = []
        for j in range(2):
            mine = low if j == 0 else jnp.logical_not(low)
            scores = dot(jnp.where(mine, q, 0.0).astype(BF16), k, TRANS_B) * temper[temper_at + 2 * p + j]
            weights = jnp.exp(scores)
            if allowed is not None:
                weights = weights * allowed
            chance = weights * (1.0 / jnp.sum(weights, axis=-1, keepdims=True))
            chances[first + 2 * p + j] = chance
            mixes.append(dot(chance.astype(BF16), v))
        mixed[rows, pl.ds(pl.multiple_of(p * 128, 128), 128)] = jnp.where(low, mixes[0], mixes[1]).astype(BF16)
        return carry

    lax.fori_loop(start, stop, pair, 0, unroll=2)


def attend_backward(act, grad_mixed, grad_act, chances, rows, first, temper, temper_at, heads):
    low = half_mask(NWIN)

    def pair(p, carry):
        at = head_columns(p, heads)
        q, k, v = (act[rows, s].astype(F32) for s in at)
        q_scale = lax.rsqrt(half_sums(q * q, low) + UNIT_EPS)
        k_scale = lax.rsqrt(half_sums(k * k, low) + UNIT_EPS)
        q, k = q * q_scale, k * k_scale
        q_low, k_low = q.astype(BF16), k.astype(BF16)
        grad = grad_mixed[rows, pl.ds(pl.multiple_of(p * 128, 128), 128)]
        gq, gk, gv = [], [], []
        for j in range(2):
            mine = low if j == 0 else jnp.logical_not(low)
            chance = chances[first + 2 * p + j]
            gc = dot(grad, jnp.where(mine, v, 0.0).astype(BF16), TRANS_B)
            gc = chance * (gc - jnp.sum(gc * chance, axis=-1, keepdims=True))
            gs = (gc * temper[temper_at + 2 * p + j]).astype(BF16)
            gq.append(dot(gs, k_low))
            gk.append(dot(gs, q_low, TRANS_A))
            gv.append(dot(chance.astype(BF16), grad, TRANS_A))
        gq, gk, gv = (jnp.where(low, *parts) for parts in (gq, gk, gv))
        grad_act[rows, at[0]] = (q_scale * (gq - q * half_sums(gq * q, low))).astype(BF16)
        grad_act[rows, at[1]] = (k_scale * (gk - k * half_sums(gk * k, low))).astype(BF16)
        grad_act[rows, at[2]] = gv.astype(BF16)
        return carry

    lax.fori_loop(0, 4, pair, 0, unroll=4)


WEIGHTS = (
    ("fk", 16, 512, "x", 512),
    ("fo", 16, 512, "x", 0),
    ("fq", 16, 512, "y", 0),
    ("fv", 16, 512, "y", 1024),
    ("mwa", 64, 512, "x", 0),
    ("mwb", 64, 512, "y", 512),
    ("cq", 32, 1536, "z", None),
    ("co", 32, 1024, "x", 0),
    ("spa", 32, 1024, "x", 0),
    ("spb", 32, 1024, "y", 1024),
)
FINE = ("fk", "fo", "fq", "fv")
SEMS_PER_WEIGHT = 33


def kernel(
    x_ref, g_ref, marks_ref, temper_fine, temper_coarse, gain_fine, gain_merge, gain_coarse,
    fq_in, fo_in, mw_in, cq_in, co_in, sp_in,
    to_merged, from_merged, send_table, region_table, back_table, halo_table,
    out_ref, gin_ref,
    fk, fo, fq, fv, mwa, mwb, cq, co, spa, spb,
    buf0, buf1, buf2, buf3, sbuf0, sbuf1, sbuf2, sbuf3,
    prx, pry, prz, prw, psx, psy, psz, psw,
    xm_ref, act, mixed, gact, chances, hid, cact, cmixed, cchances, coarse_ref, cnext_ref, gnext_ref, mn_ref, wide_ref, gh_ref,
    sems, halo_sems, pair_sems,
):
    lat, lon = lax.axis_index("lat"), lax.axis_index("lon")
    y, x_lo = lat // 2, lat % 2
    z, x_hi, core = lon // 4, (lon // 2) % 2, lon % 2

    def at_lat(by):
        return lax.rem(lat + 8 + by, 8)

    def at_lon(by):
        return lax.rem(lon + 32 + by, 32)

    z_next, z_prev = (lat, at_lon(4)), (lat, at_lon(-4))
    y_next, y_prev = (at_lat(2), lon), (at_lat(-2), lon)
    x = 2 * x_hi + x_lo

    def at_x(by):
        there = lax.rem(x + 4 + by, 4)
        return (2 * y + lax.rem(there, 2), 4 * z + 2 * (there // 2) + core)

    x_next, x_prev = at_x(1), at_x(-1)
    x_mate = (lat + 1 - 2 * x_lo, lon + 2 - 4 * x_hi)
    sibling = (lat, lon + 1 - 2 * core)
    pair_mate = (lat + 1 - 2 * x_lo, lon)
    behind = ((at_lat(-1), lon), (lat, at_lon(-1)), (at_lat(-1), at_lon(-1)))
    ahead = ((at_lat(1), lon), (lat, at_lon(1)), (at_lat(1), at_lon(1)))
    z_all = tuple((lat, at_lon(4 * by)) for by in range(1, 8))
    friends = z_all + (y_next, y_prev, x_next, x_prev, x_mate) + behind + ahead

    unfinished = []

    def send(src, dst, sem_out, sem_in, device):
        copy = pltpu.make_async_remote_copy(
            src_ref=src, dst_ref=dst, send_sem=sem_out, recv_sem=sem_in, device_id=device, device_id_type=MESH
        )
        copy.start()
        return copy

    def arrived(dst, sem_out, sem_in, device):
        pltpu.make_async_remote_copy(
            src_ref=dst, dst_ref=dst, send_sem=sem_out, recv_sem=sem_in, device_id=device, device_id_type=MESH
        ).wait_recv()

    inputs = (fq_in, fo_in, fq_in, fq_in, mw_in, mw_in, cq_in, co_in, sp_in, sp_in)
    buffers = (fk, fo, fq, fv, mwa, mwb, cq, co, spa, spb)

    def weight_events(index):
        name, rows, cols, axis, base = WEIGHTS[index]
        src, whole = inputs[index], buffers[index]
        by_x, by_z = axis == "x", axis == "z"
        width = {"x": cols // 2, "y": cols // 4, "z": cols}[axis]
        at, after, before = (x, x_next, x_prev) if by_x else (y, y_next, y_prev)
        sem = [sems.at[index, i] for i in range(SEMS_PER_WEIGHT)]

        def lanes(part):
            return pl.ds(pl.multiple_of(part * width, 128), width)

        def piece(by, levels):
            there = lax.rem(at + 4 + by, 4)
            if by_z:
                return whole.at[levels, :, core]
            if by_x:
                return whole.at[levels, there // 2, core, :, lanes(lax.rem(there, 2))]
            return whole.at[levels, :, core, :, lanes(there)]

        def block(zz):
            return piece(0, zz)

        def source(parity):
            if by_z:
                return [
                    (pl.ds(pl.multiple_of(t * 1024 + parity * 512, 128), 512), pl.ds(t * 512, 512)) for t in range(3)
                ]
            part = x_lo if by_x else y
            return [(pl.ds(pl.multiple_of(base + part * width, 128), width), lanes(part))]

        def stage_local():
            for t, (from_at, to_at) in enumerate(source(x_lo)):
                pltpu.make_async_copy(src.at[:, from_at], whole.at[z, x_hi, core, :, to_at], sem[t]).start()

        def stage_swap():
            if by_x:
                return
            for t, (from_at, to_at) in enumerate(source(1 - x_lo)):
                unfinished.append(send(
                    src.at[:, from_at], whole.at[z, x_hi, core, :, to_at], sem[3 + t], sem[6 + t], x_mate
                ))

        def forward(step):
            zz = lax.rem(z + 8 - step, 8)
            if step < 4:
                unfinished.append(send(block(zz), block(zz), sem[9 + step], sem[13 + step], z_next))

        def backward(step):
            zz = lax.rem(z + step, 8)
            if step < 3:
                unfinished.append(send(block(zz), block(zz), sem[17 + step], sem[20 + step], z_prev))

        def to_core(ref):
            send(ref, ref, sem[23], sem[24], sibling)

        def first():
            for t, (from_at, to_at) in enumerate(source(x_lo)):
                part = whole.at[z, x_hi, core, :, to_at]
                pltpu.make_async_copy(part, part, sem[t]).wait()
                if not by_x:
                    arrived(whole.at[z, 1 - x_hi, core, :, to_at], sem[3 + t], sem[6 + t], x_mate)
            if name in FINE:
                for by in (4, 3, 5, 2, 6, 1, 7):
                    unfinished.append(send(block(z), block(z), sem[8 + by], sem[15 + by], (lat, at_lon(4 * by))))
                return
            forward(0)
            backward(0)
            if by_z:
                to_core(block(z))

        def along():
            mine = piece(0, slice(None))
            unfinished.append(send(mine, mine, sem[25], sem[26], after))
            unfinished.append(send(mine, mine, sem[27], sem[28], before))
            to_core(mine)

        def collect():
            for by in (1, 7, 2, 6, 3, 5, 4):
                arrived(block(lax.rem(z + 8 - by, 8)), sem[8 + by], sem[15 + by], z_next)
            along()

        def ring(step):
            zz = lax.rem(z + 8 - step, 8)
            arrived(block(zz), sem[9 + step - 1], sem[13 + step - 1], z_next)
            forward(step)
            if by_z:
                to_core(block(zz))
            if step < 4:
                zz = lax.rem(z + step, 8)
                arrived(block(zz), sem[17 + step - 1], sem[20 + step - 1], z_prev)
                backward(step)
                if by_z:
                    to_core(block(zz))
            elif not by_z:
                along()

        low, high = pl.ds(0, 4), pl.ds(4, 4)

        def second():
            theirs = piece(-1, slice(None))
            arrived(theirs, sem[25], sem[26], after)
            unfinished.append(send(piece(-1, low), piece(-1, low), sem[29], sem[30], after))
            to_core(theirs)
            theirs = piece(1, slice(None))
            arrived(theirs, sem[27], sem[28], before)
            unfinished.append(send(piece(1, high), piece(1, high), sem[31], sem[32], before))
            to_core(theirs)

        def third():
            arrived(piece(2, low), sem[29], sem[30], after)
            arrived(piece(2, high), sem[31], sem[32], before)
            to_core(piece(2, slice(None)))

        def ready():
            arrived(whole.at[:, :, 1 - core], sem[23], sem[24], sibling)

        def sent():
            pltpu.make_async_remote_copy(
                src_ref=whole.at[:, :, core], dst_ref=whole.at[:, :, core], send_sem=sem[23], recv_sem=sem[24],
                device_id=sibling, device_id_type=MESH,
            ).wait_send()

        steps = [first] + ([collect] if name in FINE else [functools.partial(ring, s) for s in range(1, 5)])
        if not by_z:
            steps += [second, third]
        return {"local": stage_local, "swap": stage_swap, "steps": steps, "ready": ready, "sent": sent}

    events = [weight_events(i) for i in range(len(WEIGHTS))]
    place = {spec[0]: i for i, spec in enumerate(WEIGHTS)}
    done = [0] * len(WEIGHTS)

    def advance(*names):
        for name in names:
            index = place[name]
            if done[index] < len(events[index]["steps"]):
                events[index]["steps"][done[index]]()
                done[index] += 1

    def finish(*names):
        for name in names:
            while done[place[name]] < len(events[place[name]]["steps"]):
                advance(name)
        for name in names:
            events[place[name]]["ready"]()

    def halo_send(number, table, rows_from, buffer, staging, devices):
        staging[...] = dot(table[...], rows_from).astype(BF16)
        for i, (at, count) in enumerate(PIECES):
            unfinished.append(send(
                staging.at[pl.ds(at, count)], buffer.at[pl.ds(NTOK + at, count)],
                halo_sems.at[number, i], halo_sems.at[number, 3 + i], devices[i],
            ))

    def halo_wait(number, buffer, devices):
        for i, (at, count) in enumerate(PIECES):
            arrived(buffer.at[pl.ds(NTOK + at, count)], halo_sems.at[number, i], halo_sems.at[number, 3 + i], devices[i])

    def pair_send(number, values, staging, buffer):
        staging[...] = jnp.concatenate([values, jnp.zeros((PAD - NMINE, values.shape[1]), F32)], axis=0).astype(BF16)
        unfinished.append(send(staging, buffer, pair_sems.at[number, 0], pair_sems.at[number, 1], pair_mate))

    def pair_wait(number, buffer):
        arrived(buffer, pair_sems.at[number, 0], pair_sems.at[number, 1], pair_mate)
        return buffer[...].astype(F32)[:NMINE]

    for event in events:
        event["local"]()
    barrier = pltpu.get_barrier_semaphore()
    for friend in friends:
        pl.semaphore_signal(barrier, inc=1, device_id=friend, device_id_type=MESH)
    xm = dot(to_merged[...], x_ref[...]).astype(BF16)
    xm_ref[...] = xm
    for buffer in (buf0, buf1, buf2, buf3):
        buffer[pl.ds(NTOK + HALO, NCAT - NTOK - HALO), :] = jnp.zeros((NCAT - NTOK - HALO, 512), BF16)
    buf0[pl.ds(0, NTOK), :] = xm
    pl.semaphore_wait(barrier, len(friends))
    for event in events[:4]:
        event["swap"]()
    halo_send(0, send_table, xm, buf0, sbuf0, behind)
    for event in events[4:]:
        event["swap"]()
    advance(*FINE)
    gm = dot(to_merged[...], g_ref[...]).astype(BF16)
    allowed = [dot(marks_ref[w], marks_ref[w], TRANS_B) for w in range(2)]
    advance(*FINE)
    advance("mwa", "mwb", "co")
    halo_wait(0, buf0, behind)
    region = dot(region_table[...], buf0[...])
    unit, _ = normalise(region)
    region = (unit * gain_fine[...]).astype(BF16)
    advance(*FINE)
    advance("mwa", "mwb", "co")
    advance(*FINE)
    advance("mwa", "mwb", "co", "cq")
    finish("fq", "fk", "fv")

    def all_rows(ref, columns=slice(None)):
        value = ref[:, :, :, :, columns]
        return value.reshape(-1, value.shape[-1])

    for t, weight in enumerate((fq, fk, fv)):
        act[:, pl.ds(t * 512, 512)] = dot(region, all_rows(weight)).astype(BF16)
    advance("mwa", "mwb", "co")
    heads = (0, 128, 512)
    then = (("mwa", "mwb", "co", "spa", "spb"), ("cq", "spa", "spb"), ("spa", "spb"), ("cq", "spa", "spb"))
    for w in range(2):
        rows = pl.ds(w * NWIN, NWIN)
        for half in range(2):
            attend_forward(act, mixed, chances, rows, 8 * w, temper_fine, 0, allowed[w], heads, 2 * half, 2 * half + 2)
            advance(*then[2 * w + half])
    finish("fo")
    delta = dot(mixed[...], all_rows(fo)).astype(BF16)
    buf1[pl.ds(0, NTOK), :] = delta
    halo_send(1, halo_table, delta, buf1, sbuf1, ahead)
    advance("mwa", "mwb", "spa", "spb", "cq")
    halo_wait(1, buf1, ahead)
    hidden = (xm_ref[...].astype(F32) + dot(back_table[...], buf1[...])).astype(BF16)
    hid[...] = hidden
    advance("mwa", "mwb", "co")

    def cells(values):
        return jnp.concatenate([values[NMINE * i:NMINE * (i + 1)] for i in range(4)], axis=1)

    unit, merge_scale = normalise(cells(hidden.astype(F32)))
    wide_ref[...] = unit
    mn_ref[...] = (unit * gain_merge[...]).astype(BF16)
    finish("mwa", "mwb")

    for n, weight in enumerate((mwa, mwb)):
        for half in range(2):
            part = pl.ds(half * 256, 256)
            coarse_ref[:, pl.ds(n * 512 + half * 256, 256)] = dot(mn_ref[...], all_rows(weight, part)).astype(BF16).astype(F32)
    advance("cq", "co", "spa", "spb")
    coarse = coarse_ref[...]
    coarse_unit, coarse_scale = normalise(coarse)
    coarse_norm = (coarse_unit * gain_coarse[...]).astype(BF16).astype(F32)
    pair_send(0, coarse_norm, psx, prx)
    advance("spa", "spb", "co")
    grad_cells = cells(gm.astype(F32)).astype(BF16)
    finish("cq")
    mine = [dot(coarse_norm.astype(BF16), all_rows(cq, pl.ds(t * 512, 512))) for t in range(3)]
    theirs = pair_wait(0, prx).astype(BF16)
    for t in range(3):
        part = pl.ds(t * 512, 512)
        cact[:, part] = jnp.concatenate([mine[t], dot(theirs, all_rows(cq, part))], axis=0).astype(BF16)
    for half in range(2):
        attend_forward(
            cact, cmixed, cchances, pl.ds(0, NWIN), 0, temper_coarse, 8 * x_lo, None, heads, 2 * half, 2 * half + 2
        )
        advance("co", "spa", "spb")
    finish("co")
    co_mine = co[pl.ds(4 * x_lo, 4)].reshape(512, 1024)
    mix = cmixed[...].astype(F32)
    pair_send(1, dot(mix[NMINE:].astype(BF16), co_mine), psy, pry)
    partial = dot(mix[:NMINE].astype(BF16), co_mine)
    finish("spa", "spb")

    def grad_step(n, carry):
        total = dot(grad_cells[:, :1024], spa[pl.ds(2 * n, 2)].reshape(256, 1024), TRANS_B)
        total += dot(grad_cells[:, 1024:], spb[pl.ds(2 * n, 2)].reshape(256, 1024), TRANS_B)
        gnext_ref[:, pl.ds(pl.multiple_of(n * 256, 256), 256)] = total.astype(BF16).astype(F32)
        return carry

    lax.fori_loop(0, 4, grad_step, 0, unroll=True)
    grad_next = gnext_ref[...]
    pair_send(2, grad_next, psz, prz)
    coarse_next = (coarse + (partial + pair_wait(1, pry))).astype(BF16)
    cnext_ref[...] = coarse_next

    for q in range(4):
        part = pl.ds(q % 2 * 512, 512)
        rows = pl.ds(q * NMINE, NMINE)
        wide_part = dot(cnext_ref[...], all_rows((spa, spb)[q // 2], part))
        gh_ref[rows, :] = hid[rows, :].astype(F32) + wide_part
    out_ref[...] = dot(from_merged[...], gh_ref[...].astype(BF16)).astype(BF16)

    grad_window = jnp.concatenate([grad_next, pair_wait(2, prz)], axis=0).astype(BF16)
    mixed[pl.ds(0, NWIN), :] = dot(grad_window, co_mine, TRANS_B).astype(BF16)
    attend_backward(cact, mixed, gact, cchances, pl.ds(0, NWIN), 0, temper_coarse, 8 * x_lo, heads)
    grad_act = gact[pl.ds(0, NWIN), :].astype(F32)

    def through_cq(rows):
        return jnp.concatenate([dot(rows, cq[pl.ds(2 * n, 2)].reshape(256, 1536), TRANS_B) for n in range(4)], axis=1)

    pair_send(3, through_cq(grad_act[NMINE:].astype(BF16)), psw, prw)
    partial = through_cq(grad_act[:NMINE].astype(BF16))
    grad_norm = (partial + pair_wait(3, prw)).astype(BF16).astype(F32)
    grad_coarse = (grad_next + norm_back(grad_norm, gain_coarse[...], coarse_unit, coarse_scale)).astype(BF16)
    grad_merged = jnp.concatenate(
        [
            dot(grad_coarse[:, :512], mwa[n].reshape(256, 512), TRANS_B)
            + dot(grad_coarse[:, 512:], mwb[n].reshape(256, 512), TRANS_B)
            for n in range(8)
        ],
        axis=1,
    ).astype(BF16).astype(F32)
    grad_merged = norm_back(grad_merged, gain_merge[...], wide_ref[...], merge_scale).astype(BF16).astype(F32)
    for q in range(4):
        rows = pl.ds(q * NMINE, NMINE)
        gh_ref[rows, :] = grad_merged[:, q * 512:(q + 1) * 512]
    grad_hidden = (gm.astype(F32) + gh_ref[...]).astype(BF16)
    hid[...] = grad_hidden

    buf2[pl.ds(0, NTOK), :] = grad_hidden
    halo_send(2, send_table, grad_hidden, buf2, sbuf2, behind)
    halo_wait(2, buf2, behind)
    grad_region = dot(region_table[...], buf2[...]).astype(BF16)
    mixed[...] = dot(grad_region, all_rows(fo), TRANS_B).astype(BF16)
    for w in range(2):
        attend_backward(act, mixed, gact, chances, pl.ds(w * NWIN, NWIN), 8 * w, temper_fine, 0, heads)
    grad_region = sum(
        dot(gact[:, pl.ds(t * 512, 512)], all_rows(weight), TRANS_B) for t, weight in enumerate((fq, fk, fv))
    ).astype(BF16)
    buf3[pl.ds(0, NTOK), :] = grad_region
    halo_send(3, halo_table, grad_region, buf3, sbuf3, ahead)
    unit, scale = normalise(xm_ref[...].astype(F32))
    halo_wait(3, buf3, ahead)
    grad_norm = dot(back_table[...], buf3[...]).astype(BF16).astype(F32)
    grad_in = hid[...].astype(F32) + norm_back(grad_norm, gain_fine[...], unit, scale)
    gin_ref[...] = dot(from_merged[...], grad_in.astype(BF16)).astype(BF16)

    for copy in unfinished:
        copy.wait_send()
    for event in events:
        event["sent"]()


def per_device(
    fine_tokens, grad_out, window_class, temper_fine, temper_coarse, gain_fine, fine_qkv, fine_out, gain_merge,
    merge_weight, gain_coarse, coarse_qkv, coarse_out, split_weight,
):
    at_pole = (lax.axis_index("lat") == lax.axis_size("lat") - 1) & (jnp.arange(ROWS) >= 3)
    labels = window_class + 3 * at_pole.astype(jnp.int32)[None, :, None]
    labels = labels.reshape(LEV, ROWS, 2, 12).transpose(2, 0, 1, 3).reshape(2, NWIN)
    marks = (labels[:, :, None] == jnp.arange(128)[None, None, :]).astype(BF16)
    vmem = pl.BlockSpec(memory_space=pltpu.VMEM)
    smem = pl.BlockSpec(memory_space=pltpu.SMEM)
    anyplace = pl.BlockSpec(memory_space=pl.ANY)
    scratch = [pltpu.VMEM((8, 2, 2, rows, cols), BF16) for _, rows, cols, _, _ in WEIGHTS]
    scratch += [pltpu.VMEM((NCAT, 512), BF16)] * 4 + [pltpu.VMEM((HALO, 512), BF16)] * 4
    scratch += [pltpu.VMEM((PAD, 1024), BF16)] * 8
    scratch += [
        pltpu.VMEM((NTOK, 512), BF16),
        pltpu.VMEM((NTOK, 1536), BF16),
        pltpu.VMEM((NTOK, 512), BF16),
        pltpu.VMEM((NTOK, 1536), BF16),
        pltpu.VMEM((16, NWIN, NWIN), F32),
        pltpu.VMEM((NTOK, 512), BF16),
        pltpu.VMEM((NWIN, 1536), BF16),
        pltpu.VMEM((NWIN, 512), BF16),
        pltpu.VMEM((8, NWIN, NWIN), F32),
        pltpu.VMEM((NMINE, 1024), F32),
        pltpu.VMEM((NMINE, 1024), BF16),
        pltpu.VMEM((NMINE, 1024), F32),
        pltpu.VMEM((NMINE, 2048), BF16),
        pltpu.VMEM((NMINE, 2048), F32),
        pltpu.VMEM((NTOK, 512), F32),
        pltpu.SemaphoreType.DMA((len(WEIGHTS), SEMS_PER_WEIGHT)),
        pltpu.SemaphoreType.DMA((4, 6)),
        pltpu.SemaphoreType.DMA((4, 2)),
    ]
    tables = layout_tables()
    output, grad_in = pl.pallas_call(
        kernel,
        out_shape=[jax.ShapeDtypeStruct((NTOK, 512), BF16)] * 2,
        in_specs=[vmem] * 3 + [smem] * 2 + [vmem] * 3 + [anyplace] * 6 + [vmem] * 6,
        out_specs=[vmem] * 2,
        scratch_shapes=scratch,
        compiler_params=pltpu.CompilerParams(
            collective_id=0, has_side_effects=True, vmem_limit_bytes=56 * 1024 * 1024
        ),
    )(
        fine_tokens.reshape(NTOK, 512), grad_out.reshape(NTOK, 512), marks, temper_fine, temper_coarse,
        gain_fine.reshape(1, -1), gain_merge.reshape(1, -1), gain_coarse.reshape(1, -1),
        fine_qkv, fine_out, merge_weight, coarse_qkv, coarse_out, split_weight, *tables,
    )
    return output.reshape(fine_tokens.shape), grad_in.reshape(fine_tokens.shape)


def solution(mesh):
    tiles = P(None, "lat", "lon", None)
    shards = P("lon", None)
    return jax.shard_map(
        per_device,
        mesh=mesh,
        in_specs=(
            tiles, tiles, P(None, "lat", "lon"), P(), P(), P(), shards, shards, P(), shards, P(), shards, shards, shards,
        ),
        out_specs=(tiles, tiles),
        check_vma=False,
    )
```
